256 devices in a mesh: pipe: 8 (over z_hi, core), expert: 8 (over x, z_lo), tensor: 4 (over y).
Axes of the slice: x: 4, y: 4, z: 8 (z_hi: 4, z_lo: 2; z = z_hi * 2 + z_lo), core: 2. Of those that a mesh axis runs over, the one named last changes fastest.
Arguments:
- stream: bfloat16 [8, 2, 512, 4096], P('pipe', None, 'expert', 'tensor'), may hold values from -6 to 6
- expert_ids: int32 [8, 2, 512, 2], P('pipe', None, 'expert'), may hold values from 0 to 7, all different within a row; in each aligned block of 64 rows (0 to 63, 64 to 127, ..., all dimensions but the last counted through in order) at most 32 rows name the same one
- expert_gates: float32 [8, 2, 512, 2], P('pipe', None, 'expert'), may hold values from 0.1 to 1
- moe_gain: bfloat16 [8, 4096], P('pipe', 'tensor'), may hold values from 0.5 to 1.5
- w_gate: bfloat16 [8, 8, 4096, 1536], P('pipe', 'expert', None, 'tensor'), may hold values from -0.09375 to 0.09375
- w_up: bfloat16 [8, 8, 4096, 1536], P('pipe', 'expert', None, 'tensor'), may hold values from -0.09375 to 0.09375
- w_down: bfloat16 [8, 8, 1536, 4096], P('pipe', 'expert', 'tensor'), may hold values from -0.15625 to 0.15625
- attn_gain: bfloat16 [8, 4096], P('pipe', 'tensor'), may hold values from 0.5 to 1.5
- w_query: bfloat16 [8, 4096, 512], P('pipe', None, 'tensor'), may hold values from -3 to 3
- w_keyval: bfloat16 [8, 4096, 2, 512], P('pipe', None, None, 'tensor'), may hold values from -3 to 3
Outputs:
- moe_out: bfloat16 [8, 2, 512, 4096], P('pipe', None, 'expert', 'tensor')
- context: bfloat16 [8, 2, 512, 512], P('pipe', None, 'expert', 'tensor')
The draws below stay inside these ranges and needn't reach their ends.
Inputs may be any that keep to these rules, and one draw needn't show every extreme that they name: `expert_ids`: in each aligned block of 64 positions of one sequence (the positions of one device), at most 32 positions name one expert; the two experts of a position differ.
All inputs are finite; a program needn't handle non-finite values.
Results may differ from the reference program's by a relative error of at most 0.02.
The reference program's roundings to bfloat16 on the way count: a program that leaves them out, or rounds other values in their place, can miss the bound.
Values may be sent and summed in bfloat16 or wider, within the bound.
A program may use at most 64 MiB of HBM per device.

```python
import math
import jax
import jax.numpy as jnp
import numpy as np
from jax import lax

D = 4096
HS = 128
GROUP = 1
MICRO = 2
SEQ_DEV = 64
EXPERTS = 8
FF = 1536
QHEADS = 4
KVHEADS = 4
SEQ = 512
SECTIONS = 8
CAPM = 32
N_EXPERT = 8


def draw_w_query(key, part):
    own = jax.random.fold_in(key, 11)
    noise_key = jax.random.fold_in(own, 0)
    base = jnp.clip(jax.random.normal(noise_key, (SECTIONS, D, KVHEADS, GROUP, HS), jnp.float32), -6.0, 6.0) / math.sqrt(D)
    return base.reshape(SECTIONS, D, QHEADS * HS).astype(jnp.bfloat16)


def draw_w_keyval(key, part):
    own = jax.random.fold_in(key, 23)
    noise_key = jax.random.fold_in(own, 0)
    base = jnp.clip(jax.random.normal(noise_key, (SECTIONS, D, 2, KVHEADS, HS), jnp.float32), -6.0, 6.0) / math.sqrt(D)
    return base.reshape(SECTIONS, D, 2, KVHEADS * HS).astype(jnp.bfloat16)


def level_of(key, shape, shards, least, top_value):
    factor_of = 1.0
    for position, shards_of in shards:
        steps = jax.random.uniform(jax.random.fold_in(jax.random.fold_in(key, 6), position), (shards_of,), jnp.float32, least / len(shards), top_value / len(shards))
        factor_of = factor_of * jnp.repeat(jnp.exp(steps), shape[position] // shards_of).reshape((-1,) + (1,) * (len(shape) - 1 - position))
    return factor_of


def deal_out(stream_key, own, number, rows, amount, top, reach, skew):
    sequence = jax.random.permutation(stream_key, amount)
    heavy_load, ordinary = load_shares(amount, rows * top, reach, skew, True), load_shares(amount, rows * top, reach, skew, False)
    places = jnp.arange(amount)

    def named(tallies, offset_by):
        used = int((tallies > 0).sum())
        fixed = max(1, used // 4)
        passed = fixed + (places - fixed + offset_by * (used - fixed)) % max(1, amount - fixed)
        return jnp.zeros((amount,), jnp.int32).at[sequence[jnp.where(places < fixed, places, passed)]].set(jnp.asarray(tallies, jnp.int32))

    tallies = jnp.where(number % 4 == 0, named(heavy_load, number // 4), named(ordinary, number - number // 4 - 1))
    mixed = jax.random.permutation(jax.random.fold_in(own, 3), amount)
    source_of, receiver = mixed[0:amount // 2 * 2:2], mixed[1:amount // 2 * 2:2]
    slack = jnp.minimum(tallies[source_of] - 1, reach - tallies[receiver]) // 2
    slack = jnp.where((source_of == sequence[0]) | (receiver == sequence[0]) | (tallies[receiver] == 0), 0, jnp.maximum(slack, 0))
    passed = jax.random.randint(jax.random.fold_in(own, 4), (amount // 2,), 0, 1 << 20) % (slack + 1)
    tallies = tallies.at[source_of].add(-passed).at[receiver].add(passed)
    labels = jnp.searchsorted(jnp.cumsum(tallies), jnp.arange(rows * top), side="right").astype(jnp.int32)
    listing = labels.reshape(top, rows).T
    listing = listing[jax.random.permutation(jax.random.fold_in(own, 1), rows)]
    offset_by = jax.random.randint(jax.random.fold_in(own, 2), (rows, 1), 0, top)
    return jnp.take_along_axis(listing, (jnp.arange(top)[None, :] + offset_by) % top, axis=1)


def load_shares(amount, total, most, slope, full):
    portions = [(1 << 20) // math.isqrt(grade ** slope) + 1 for grade in range(1, amount + 1)]
    largest = most if full else min(most, max(-(-total // amount), total * portions[0] // sum(portions)))
    least = 1 if total - largest >= amount - 1 else 0
    holding, surplus = [largest] + [least] * (amount - 1), total - largest - least * (amount - 1)
    while surplus > 0:
        movable = [i for i in range(1, amount) if holding[i] < largest] or [i for i in range(1, amount) if holding[i] < most]
        whole, budget = sum([portions[i] for i in movable]), surplus
        for i in movable:
            more = min(most - holding[i], max(1, budget * portions[i] // whole), surplus)
            holding[i] = holding[i] + more
            surplus = surplus - more
    return np.array(holding)


def centred(own_key, dims, deviation, reach, cuts=(), held_as=jnp.bfloat16):
    factor_of = level_of(own_key, dims, cuts, -0.22, 0.18) if cuts else 1.0
    array = jax.random.normal(own_key, dims, jnp.float32) * deviation * factor_of
    return jnp.minimum(jnp.maximum(array, -reach), reach).astype(held_as)


def setup_inputs(seed: int = 0) -> dict:
    streams_of = jax.random.split(jax.random.key(seed), 11)
    stream = centred(streams_of[0], (SECTIONS, MICRO, SEQ, D), 1.0, 6.0, ((0, 8), (2, 8), (3, 4)))
    expert_ids_keys = jax.random.split(jax.random.fold_in(streams_of[1], 1), SECTIONS * MICRO * SEQ // SEQ_DEV)
    expert_ids_turns = jax.random.permutation(jax.random.fold_in(streams_of[1], 3), SECTIONS * MICRO * SEQ // SEQ_DEV)
    expert_ids = jax.vmap(lambda own, number: deal_out(jax.random.fold_in(streams_of[1], 2), own, number, SEQ_DEV, EXPERTS, 2, CAPM, 2))(expert_ids_keys, expert_ids_turns).reshape((SECTIONS, MICRO, SEQ, 2))
    expert_gates = jnp.clip(0.1 + 0.9 * jax.random.uniform(streams_of[2], (SECTIONS, MICRO, SEQ, 2), jnp.float32) ** level_of(streams_of[2], (SECTIONS, MICRO, SEQ, 2), ((0, 8), (2, 8)), -0.2, 0.2), 0.1, 1.0)
    moe_gain = jnp.clip(1.0 + 0.1 * jax.random.normal(streams_of[3], (SECTIONS, D), jnp.float32), 0.5, 1.5).astype(jnp.bfloat16)
    w_gate = centred(streams_of[4], (SECTIONS, EXPERTS, D, FF), D ** -0.5, 0.09375, ((0, 8), (1, 8), (3, 4)))
    w_up = centred(streams_of[5], (SECTIONS, EXPERTS, D, FF), D ** -0.5, 0.09375, ((0, 8), (1, 8), (3, 4)))
    w_down = centred(streams_of[6], (SECTIONS, EXPERTS, FF, D), FF ** -0.5, 0.15625, ((0, 8), (1, 8), (2, 4)))
    attn_gain = jnp.clip(1.0 + 0.1 * jax.random.normal(streams_of[7], (SECTIONS, D), jnp.float32), 0.5, 1.5).astype(jnp.bfloat16)
    w_query = draw_w_query(jax.random.fold_in(streams_of[10], 71), 0)
    w_keyval = draw_w_keyval(jax.random.fold_in(streams_of[10], 71), 0)
    return dict(stream=stream, expert_ids=expert_ids, expert_gates=expert_gates, moe_gain=moe_gain, w_gate=w_gate, w_up=w_up, w_down=w_down, attn_gain=attn_gain, w_query=w_query, w_keyval=w_keyval)


EPS = 1e-05
THETA = 1000000.0
NEGATIVE = -1e+30

def rms_scale(values, gain):
    floats = values.astype(jnp.float32)
    meansq = lax.optimization_barrier(jnp.mean(floats * floats, axis=-1, keepdims=True))
    return (floats * lax.rsqrt(meansq + EPS) * gain.astype(jnp.float32)).astype(jnp.bfloat16)

def rotate(values, positions):
    heads = values.shape[-1] // HS
    shaped = values.reshape(values.shape[:-1] + (heads, HS))
    half_size = HS // 2
    freqs = jnp.exp(-jnp.log(THETA) * jnp.arange(half_size, dtype=jnp.float32) * 2.0 / HS)
    angles = positions[:, None] * freqs[None, :]
    cosine = jnp.cos(angles)[:, None, :]
    sine = jnp.sin(angles)[:, None, :]
    first = shaped[..., :half_size]
    second = shaped[..., half_size:]
    turned = jnp.concatenate([first * cosine - second * sine, second * cosine + first * sine], axis=-1)
    return turned.reshape(values.shape)

def moe_section(stream, expert_ids, expert_gates, moe_gain, w_gate, w_up, w_down):
    normed = rms_scale(stream, moe_gain)
    blocks = N_EXPERT
    seq_dev = SEQ // blocks
    ids_block = expert_ids.reshape(MICRO, blocks, seq_dev * 2)
    onehot = (ids_block[..., None] == jnp.arange(EXPERTS, dtype=jnp.int32)).astype(jnp.int32)
    ranks = jnp.cumsum(onehot, axis=2) - onehot
    slots = lax.optimization_barrier(jnp.sum(ranks * onehot, axis=-1)).astype(jnp.int32)
    row_values = jnp.repeat(normed.reshape(MICRO, blocks, seq_dev, D), 2, axis=2)
    micro_index = jnp.arange(MICRO, dtype=jnp.int32)[:, None, None]
    block_index = jnp.arange(blocks, dtype=jnp.int32)[None, :, None]
    buffer = jnp.zeros((MICRO, blocks, EXPERTS, CAPM, D), jnp.bfloat16)
    buffer = buffer.at[micro_index, block_index, ids_block, slots].set(row_values)

    def one_expert(index):
        inputs = buffer[:, :, index].reshape(-1, D)
        gated = jnp.dot(inputs, w_gate[index], preferred_element_type=jnp.float32)
        lifted = jnp.dot(inputs, w_up[index], preferred_element_type=jnp.float32)
        hidden = (jax.nn.silu(gated) * lifted).astype(jnp.bfloat16)
        result = jnp.dot(hidden, w_down[index], preferred_element_type=jnp.float32).astype(jnp.bfloat16)
        return result.reshape(MICRO, blocks, CAPM, D)
    outputs = lax.map(one_expert, jnp.arange(EXPERTS, dtype=jnp.int32))
    picked = outputs[ids_block, micro_index, block_index, slots].astype(jnp.float32)
    weighted = picked * expert_gates.reshape(MICRO, blocks, seq_dev * 2)[..., None]
    summed = lax.optimization_barrier(jnp.sum(weighted.reshape(MICRO, blocks, seq_dev, 2, D), axis=3)).reshape(MICRO, SEQ, D)
    return (stream.astype(jnp.float32) + summed).astype(jnp.bfloat16)

def attend_micro(query, keys, values):
    scores = jnp.einsum('qkgd,nkd->kgqn', query.astype(jnp.float32), keys.astype(jnp.float32)) * HS ** (-0.5)
    causal = jnp.arange(SEQ)[None, :] <= jnp.arange(SEQ)[:, None]
    scores = jnp.where(causal, scores, NEGATIVE)
    highest = lax.optimization_barrier(jnp.max(scores, axis=-1, keepdims=True))
    weights = jnp.where(causal, jnp.exp(scores - highest), 0.0)
    totals = lax.optimization_barrier(jnp.sum(weights, axis=-1))
    rounded = weights.astype(jnp.bfloat16)
    summed = jnp.einsum('kgqn,nkd->qkgd', rounded.astype(jnp.float32), values.astype(jnp.float32))
    context = summed / jnp.transpose(totals, (2, 0, 1))[..., None]
    return context.astype(jnp.bfloat16).reshape(SEQ, -1)

def attn_section(received, attn_gain, w_query, w_keyval):
    normed = rms_scale(received, attn_gain)
    flat = normed.reshape(-1, D)
    positions = jnp.arange(SEQ, dtype=jnp.float32)
    query = jnp.dot(flat, w_query, preferred_element_type=jnp.float32).reshape(MICRO, SEQ, -1)
    query = rotate(query, positions).astype(jnp.bfloat16)
    key_width = KVHEADS * HS
    keyval = jnp.dot(flat, w_keyval.reshape(D, 2 * key_width), preferred_element_type=jnp.float32)
    keyval = keyval.reshape(MICRO, SEQ, 2, key_width)
    keys = rotate(keyval[:, :, 0], positions).astype(jnp.bfloat16)
    values = keyval[:, :, 1].astype(jnp.bfloat16)
    query = query.reshape(MICRO, SEQ, KVHEADS, GROUP, HS)
    keys = keys.reshape(MICRO, SEQ, KVHEADS, HS)
    values = values.reshape(MICRO, SEQ, KVHEADS, HS)
    return lax.map(lambda pieces: attend_micro(*pieces), (query, keys, values))

def reference(stream, expert_ids, expert_gates, moe_gain, w_gate, w_up, w_down, attn_gain, w_query, w_keyval):
    moe_out = lax.map(lambda pieces: moe_section(*pieces), (stream, expert_ids, expert_gates, moe_gain, w_gate, w_up, w_down))
    received = jnp.roll(moe_out, 1, axis=0)
    context = lax.map(lambda pieces: attn_section(*pieces), (received, attn_gain, w_query, w_keyval))
    return (moe_out, context)
```

```python
import jax
import jax.numpy as jnp
import numpy as np
from jax import lax
from jax.experimental import pallas as pl
from jax.experimental.pallas import tpu as pltpu
from jax.sharding import PartitionSpec as P

MESH = pl.DeviceIdType.MESH
HS = 128
EPS = 1e-05
THETA = 1000000.0
NEGATIVE = -1e30
F32 = jnp.float32
BF16 = jnp.bfloat16
I16 = jnp.int16

MICRO = 2
ROWS = 64
PART = 1024
CAP = 32
EXPERTS = 8
SLOTS = EXPERTS * CAP
HALF = SLOTS // 2
CUTS = 2
WIDE = PART // CUTS
FF = 384
LENGTH = EXPERTS * ROWS
RIGHT, OPPOSITE, LEFT = 1, 2, 3
SEMAPHORES = 160


def rope_table(length):
    freqs = THETA ** (-2.0 * np.arange(HS // 2) / HS)
    angles = np.arange(length)[:, None] * freqs[None, :]
    cosine, sine = np.cos(angles), np.sin(angles)
    return np.concatenate([cosine, cosine, -sine, sine], axis=1).astype(np.float32)


class Group:
    def __init__(self, sem, whole):
        self.sem, self.whole, self.sent, self.waited = sem, whole, False, False


class Messages:
    def __init__(self, sems):
        self.sems, self.used, self.sends, self.recvs = sems, 0, [], []

    def group(self, whole, kind):
        found = Group(self.sems.at[self.used], whole)
        self.used += 1
        kind.append(found)
        return found

    def leaving(self, whole):
        return self.group(whole, self.sends)

    def coming(self, whole):
        return self.group(whole, self.recvs)

    def send(self, src, dst, leaving, coming, **where):
        pltpu.make_async_remote_copy(
            src_ref=src,
            dst_ref=dst,
            send_sem=leaving.sem,
            recv_sem=coming.sem,
            device_id=where,
            device_id_type=MESH,
        ).start()
        leaving.sent = coming.sent = True

    def _any(self, found):
        return pltpu.make_async_remote_copy(
            src_ref=found.whole,
            dst_ref=found.whole,
            send_sem=found.sem,
            recv_sem=found.sem,
            device_id={"tensor": lax.rem(lax.axis_index("tensor") + 1, 4)},
            device_id_type=MESH,
        )

    def wait(self, found):
        self._any(found).wait_recv()
        found.waited = True

    def finish(self):
        for found in self.recvs:
            if found.sent and not found.waited:
                self.wait(found)
        for found in self.sends:
            if found.sent:
                self._any(found).wait_send()


def dot(a, b):
    return jnp.dot(a, b, preferred_element_type=F32)


def dot_first(a, b):
    return lax.dot_general(a, b, (((0,), (0,)), ((), ())), preferred_element_type=F32)


def flipped(line):
    n = max(line.shape)
    diagonal = lax.broadcasted_iota(jnp.int32, (n, n), 0) == lax.broadcasted_iota(
        jnp.int32, (n, n), 1
    )
    axis = 0 if line.shape[1] == 1 else 1
    return jnp.sum(jnp.where(diagonal, line, 0.0), axis=axis, keepdims=True)


def encoded(value):
    highest = jnp.maximum(jnp.max(jnp.abs(value), axis=1, keepdims=True), 1e-30)
    codes = jnp.round(value * (32760.0 / highest)).astype(jnp.int32).astype(I16)
    return codes, highest * (1.0 / 32760.0)


def decoded(codes, step):
    return codes.astype(jnp.int32).astype(F32) * step


def kernel(
    stream_hbm, ids_hbm, gates_hbm, mgain_hbm, again_hbm,
    wg_hbm, wu_hbm, wd_hbm, wq_hbm, wkv_hbm, rope_hbm,
    moe_out, context_out,
    stream, ids, gates, mgain, again, w13, wd, wqkv, wkv, rope,
    ssq, gains, out, x, acc, hidden,
    opp, going_r, going_l, part_r, part_l, own, opp_l, opp_r, sum_l, sum_r,
    steps_r, steps_l, steps_from_r, steps_from_l, more_r, more_l, more_from_r, more_from_l,
    eo, ret, mixed, rows_in, kv_own, kv_in, context,
    local_sems, sems,
):
    e, t, p = lax.axis_index("expert"), lax.axis_index("tensor"), lax.axis_index("pipe")
    right, left, opposite = lax.rem(t + 1, 4), lax.rem(t + 3, 4), lax.rem(t + 2, 4)
    after, before = lax.rem(p + 1, 8), lax.rem(p + 7, 8)
    peer = [lax.rem(e + o, EXPERTS) for o in range(EXPERTS)]
    msg = Messages(sems)

    here = pl.ds(pl.multiple_of(e * ROWS, ROWS), ROWS)
    loads = [
        (stream_hbm, stream),
        (ids_hbm, ids),
        (mgain_hbm, mgain),
        (gates_hbm, gates),
        (again_hbm, again),
        (wg_hbm, w13.at[:, :FF]),
        (wu_hbm, w13.at[:, FF:]),
        (wd_hbm, wd),
        (wq_hbm, wqkv.at[:, :HS]),
        (wkv_hbm, wkv),
        (rope_hbm.at[here], rope),
    ]
    loads = [pltpu.make_async_copy(s, d, local_sems.at[i]) for i, (s, d) in enumerate(loads)]
    for load in loads:
        load.start()

    barrier = pltpu.get_barrier_semaphore()
    peers = [{"expert": other} for other in peer[1:]]
    peers += [{"tensor": other} for other in (right, left, opposite)]
    peers += [{"pipe": other} for other in (after, before)]
    for other in peers:
        pl.semaphore_signal(barrier, inc=1, device_id=other, device_id_type=MESH)

    slot = lax.broadcasted_iota(jnp.int32, (SLOTS, ROWS), 0)
    group, place = slot // CAP, slot % CAP
    expert_of = jnp.where(group + e >= EXPERTS, group + e - EXPERTS, group + e)
    row_of = lax.broadcasted_iota(jnp.int32, (ROWS, ROWS), 0)
    col_of = lax.broadcasted_iota(jnp.int32, (ROWS, ROWS), 1)
    earlier = jnp.where(row_of < col_of, 1.0, 0.0).astype(BF16)
    for load in loads[:5]:
        load.wait()
    chosen = []
    for m in range(MICRO):
        first = ids[m, 0:1, :] == expert_of
        second = ids[m, 1:2, :] == expert_of
        named = jnp.where(first | second, 1.0, 0.0)
        taken = dot(named.astype(BF16), earlier) == place.astype(F32)
        chosen.append(
            [jnp.where(which & taken, 1.0, 0.0).astype(BF16) for which in (first, second)]
        )

    value = stream[...].reshape(MICRO * ROWS, PART).astype(F32)
    ssq[0] = jnp.broadcast_to(flipped(jnp.sum(value * value, axis=1, keepdims=True)), (8, MICRO * ROWS))
    gains[0] = jnp.broadcast_to(again[...], (16, PART))

    pl.semaphore_wait(barrier, len(peers))

    def to_tensor_peers(buffer):
        leaving, coming = msg.leaving(buffer.at[1:4]), msg.coming(buffer.at[1:4])
        for rel, other in ((RIGHT, right), (LEFT, left), (OPPOSITE, opposite)):
            msg.send(buffer.at[0], buffer.at[rel], leaving, coming, tensor=other)
        return coming

    msg.wait(to_tensor_peers(ssq))
    total = (ssq[0, 0:1, :] + ssq[1, 0:1, :]) + (ssq[2, 0:1, :] + ssq[3, 0:1, :])
    scales = flipped(lax.rsqrt(total * (1.0 / (4 * PART)) + EPS))

    out_leave = [msg.leaving(out.at[m, 1:]) for m in range(MICRO)]
    out_come = [[None] + [msg.coming(x.at[m, 0, o]) for o in range(1, EXPERTS)] for m in range(MICRO)]
    x_leave_r = [msg.leaving(x.at[m, 0]) for m in range(MICRO)]
    x_leave_l = [msg.leaving(x.at[m, 0]) for m in range(MICRO)]
    near = EXPERTS // 2
    x_come_r = [
        [msg.coming(x.at[m, RIGHT, o]) for o in range(near)] + [msg.coming(x.at[m, RIGHT, near:])] * near
        for m in range(MICRO)
    ]
    x_come_l = [
        [msg.coming(x.at[m, LEFT, :near])] * near + [msg.coming(x.at[m, LEFT, o]) for o in range(near, EXPERTS)]
        for m in range(MICRO)
    ]
    ahead_leave_r = [msg.leaving(x.at[m, RIGHT, :near]) for m in range(MICRO)]
    ahead_leave_l = [msg.leaving(x.at[m, LEFT, near:]) for m in range(MICRO)]
    ahead_come_r = [msg.coming(x.at[m, OPPOSITE, :near]) for m in range(MICRO)]
    ahead_come_l = [msg.coming(x.at[m, OPPOSITE, near:]) for m in range(MICRO)]

    def place_rows(m):
        scale = scales[m * ROWS : (m + 1) * ROWS]
        normed = (stream[m].astype(F32) * scale * mgain[...].astype(F32)).astype(BF16)
        block = dot(chosen[m][0] + chosen[m][1], normed).astype(BF16).reshape(EXPERTS, CAP, PART)
        x[m, 0, 0] = block[0]
        out[m] = block

    def dispatch(m):
        for o in range(1, EXPERTS):
            msg.send(out.at[m, o], x.at[m, 0, o], out_leave[m], out_come[m][o], expert=peer[o])

    def gather_send(m, pieces):
        for o in pieces:
            if o > 0:
                msg.wait(out_come[m][o])
            msg.send(x.at[m, 0, o], x.at[m, RIGHT, o], x_leave_r[m], x_come_r[m][o], tensor=right)
            msg.send(x.at[m, 0, o], x.at[m, LEFT, o], x_leave_l[m], x_come_l[m][o], tensor=left)

    def gather_forward(m):
        for i in range(near):
            msg.wait(x_come_r[m][i])
            msg.send(x.at[m, RIGHT, i], x.at[m, OPPOSITE, i], ahead_leave_r[m], ahead_come_r[m], tensor=right)
            o = i + near
            msg.wait(x_come_l[m][o])
            msg.send(x.at[m, LEFT, o], x.at[m, OPPOSITE, o], ahead_leave_l[m], ahead_come_l[m], tensor=left)

    def quarter(rel):
        return pl.ds(pl.multiple_of(lax.rem(t + 4 - rel, 4) * PART, PART), PART)

    def expert_in(m, rel):
        value = dot(x[m, rel].reshape(SLOTS, PART), w13[quarter(rel), :])
        acc[...] = value if rel == 0 else acc[...] + value

    def activate(m):
        gated, lifted = acc[:, :FF], acc[:, FF:]
        hidden[m] = (gated / (1.0 + jnp.exp(-gated)) * lifted).astype(BF16)

    def pairs(buffer, kind):
        return [kind(buffer.at[m]) for m in range(MICRO)]

    def each(buffer, rows):
        return [[msg.coming(buffer.at[m, c, rows]) for c in range(CUTS)] for m in range(MICRO)]

    top, low, every = slice(0, HALF), slice(HALF, SLOTS), slice(None)
    opp_leave, going_r_leave, going_l_leave = (
        pairs(b, msg.leaving) for b in (opp, going_r, going_l)
    )
    steps_r_leave, steps_l_leave, more_r_leave, more_l_leave = (
        pairs(b, msg.leaving) for b in (steps_r, steps_l, more_r, more_l)
    )
    opp_l_come, opp_r_come = each(opp_l, every), each(opp_r, every)
    sum_l_top, sum_l_low = each(sum_l, top), each(sum_l, low)
    sum_r_top, sum_r_low = each(sum_r, top), each(sum_r, low)
    steps_l_come, steps_r_come = each(steps_from_l, every), each(steps_from_r, every)
    more_l_come, more_r_come = each(more_from_l, every), each(more_from_r, every)

    def part(m, c, rel):
        at = pl.multiple_of(lax.rem(t + rel, 4) * PART + c * WIDE, WIDE)
        return dot(hidden[m], wd[:, pl.ds(at, WIDE)])

    def send_opposite(m, c):
        opp[m, c], step = encoded(part(m, c, OPPOSITE))
        for ref in (steps_r, steps_l, more_r, more_l):
            ref[m, c] = jnp.zeros((8, HALF), F32)
        steps_r[m, c, 0:1] = flipped(step[:HALF])
        steps_l[m, c, 0:1] = flipped(step[HALF:])
        msg.send(opp.at[m, c, top], opp_l.at[m, c], opp_leave[m], opp_l_come[m][c], tensor=right)
        msg.send(opp.at[m, c, low], opp_r.at[m, c], opp_leave[m], opp_r_come[m][c], tensor=left)

    def send_direct(m, c):
        value = part(m, c, RIGHT)
        part_r[m, c] = value[:HALF]
        going_r[m, c, low], step = encoded(value[HALF:])
        steps_r[m, c, 1:2] = flipped(step)
        msg.send(steps_r.at[m, c], steps_from_l.at[m, c], steps_r_leave[m], steps_l_come[m][c], tensor=right)
        msg.send(going_r.at[m, c, low], sum_l.at[m, c, low], going_r_leave[m], sum_l_low[m][c], tensor=right)
        value = part(m, c, LEFT)
        part_l[m, c] = value[HALF:]
        going_l[m, c, top], step = encoded(value[:HALF])
        steps_l[m, c, 1:2] = flipped(step)
        msg.send(steps_l.at[m, c], steps_from_r.at[m, c], steps_l_leave[m], steps_r_come[m][c], tensor=left)
        msg.send(going_l.at[m, c, top], sum_r.at[m, c, top], going_l_leave[m], sum_r_top[m][c], tensor=left)

    def sum_middle(m, c):
        msg.wait(steps_l_come[m][c])
        msg.wait(opp_l_come[m][c])
        value = part_r[m, c] + decoded(opp_l[m, c], flipped(steps_from_l[m, c, 0:1]))
        going_r[m, c, top], step = encoded(value)
        more_r[m, c, 0:1] = flipped(step)
        msg.send(more_r.at[m, c], more_from_l.at[m, c], more_r_leave[m], more_l_come[m][c], tensor=right)
        msg.send(going_r.at[m, c, top], sum_l.at[m, c, top], going_r_leave[m], sum_l_top[m][c], tensor=right)
        msg.wait(steps_r_come[m][c])
        msg.wait(opp_r_come[m][c])
        value = part_l[m, c] + decoded(opp_r[m, c], flipped(steps_from_r[m, c, 0:1]))
        going_l[m, c, low], step = encoded(value)
        more_l[m, c, 0:1] = flipped(step)
        msg.send(more_l.at[m, c], more_from_r.at[m, c], more_l_leave[m], more_r_come[m][c], tensor=left)
        msg.send(going_l.at[m, c, low], sum_r.at[m, c, low], going_l_leave[m], sum_r_low[m][c], tensor=left)

    eo_leave = [msg.leaving(eo.at[m, :, 1:]) for m in range(MICRO)]
    ret_come = [[msg.coming(ret.at[m, c, 1:]) for c in range(CUTS)] for m in range(MICRO)]

    def sum_last(m, c):
        for found in (sum_l_low, sum_r_top, more_l_come, sum_l_top, more_r_come, sum_r_low):
            msg.wait(found[m][c])
        above = own[m, c, top] + (
            decoded(sum_l[m, c, top], flipped(more_from_l[m, c, 0:1]))
            + decoded(sum_r[m, c, top], flipped(steps_from_r[m, c, 1:2]))
        )
        below = own[m, c, low] + (
            decoded(sum_l[m, c, low], flipped(steps_from_l[m, c, 1:2]))
            + decoded(sum_r[m, c, low], flipped(more_from_r[m, c, 0:1]))
        )
        value = jnp.concatenate([above.astype(BF16), below.astype(BF16)], axis=0)
        value = value.reshape(EXPERTS, CAP, WIDE)
        ret[m, c, 0] = value[0]
        eo[m, c] = value
        for o in range(1, EXPERTS):
            msg.send(
                eo.at[m, c, o], ret.at[m, c, o], eo_leave[m], ret_come[m][c],
                expert=lax.rem(e + EXPERTS - o, EXPERTS),
            )

    mixed_leave = [msg.leaving(mixed.at[m]) for m in range(MICRO)]
    moe_writes = []
    shift_come = [[msg.coming(rows_in.at[m, 0, c]) for c in range(CUTS)] for m in range(MICRO)]

    def combine(m, c):
        msg.wait(ret_come[m][c])
        returned = ret[m, c].reshape(SLOTS, WIDE)
        columns = slice(c * WIDE, (c + 1) * WIDE)
        value = None
        for k in range(2):
            term = flipped(gates[m, k : k + 1, :]) * dot_first(chosen[m][k], returned)
            value = term if value is None else value + term
        mixed[m, c] = (stream[m, :, columns].astype(F32) + value).astype(BF16)
        msg.send(mixed.at[m, c], rows_in.at[m, 0, c], mixed_leave[m], shift_come[m][c], pipe=after)
        number = len(loads) + len(moe_writes)
        moe_writes.append(
            pltpu.make_async_copy(mixed.at[m, c], moe_out.at[m, :, columns], local_sems.at[number])
        )
        moe_writes[-1].start()

    half = ROWS // 2
    rows_leave_r, rows_leave_l = (
        [msg.leaving(rows_in.at[m, 0]) for m in range(MICRO)] for _ in range(2)
    )
    rows_ahead_r = [msg.leaving(rows_in.at[m, RIGHT, :, :half]) for m in range(MICRO)]
    rows_ahead_l = [msg.leaving(rows_in.at[m, LEFT, :, half:]) for m in range(MICRO)]
    rows_come_r, rows_come_l = (
        [[msg.coming(rows_in.at[m, rel, c]) for c in range(CUTS)] for m in range(MICRO)]
        for rel in (RIGHT, LEFT)
    )
    rows_far_r = [[msg.coming(rows_in.at[m, OPPOSITE, c, :half]) for c in range(CUTS)] for m in range(MICRO)]
    rows_far_l = [[msg.coming(rows_in.at[m, OPPOSITE, c, half:]) for c in range(CUTS)] for m in range(MICRO)]

    def rows_send(m, c):
        msg.wait(shift_come[m][c])
        msg.send(rows_in.at[m, 0, c], rows_in.at[m, RIGHT, c], rows_leave_r[m], rows_come_r[m][c], tensor=right)
        msg.send(rows_in.at[m, 0, c], rows_in.at[m, LEFT, c], rows_leave_l[m], rows_come_l[m][c], tensor=left)

    def rows_forward(m, c):
        msg.wait(rows_come_r[m][c])
        msg.send(
            rows_in.at[m, RIGHT, c, :half], rows_in.at[m, OPPOSITE, c, :half],
            rows_ahead_r[m], rows_far_r[m][c], tensor=right,
        )
        msg.wait(rows_come_l[m][c])
        msg.send(
            rows_in.at[m, LEFT, c, half:], rows_in.at[m, OPPOSITE, c, half:],
            rows_ahead_l[m], rows_far_l[m][c], tensor=left,
        )

    kv_leave = [msg.leaving(kv_in.at[m, 1:]) for m in range(MICRO)]
    kv_come = [msg.coming(kv_in.at[m, 1:]) for m in range(MICRO)]

    def turned(value):
        swapped = pltpu.roll(value, HS // 2, 1)
        return (value * rope[:, :HS] + swapped * rope[:, HS:]).astype(BF16)

    def project(m):
        for c in range(CUTS):
            msg.wait(rows_far_r[m][c])
            msg.wait(rows_far_l[m][c])
        total = None
        for rel in range(4):
            for c in range(CUTS):
                value = rows_in[m, rel, c].astype(F32)
                term = jnp.sum(value * value, axis=-1, keepdims=True)
                total = term if total is None else total + term
        scale = lax.rsqrt(total * (1.0 / (4 * PART)) + EPS)
        result = None
        for rel in range(4):
            for c in range(CUTS):
                gain = gains[rel, 0:1, c * WIDE : (c + 1) * WIDE].astype(F32)
                normed = (rows_in[m, rel, c].astype(F32) * scale * gain).astype(BF16)
                at = pl.multiple_of(lax.rem(t + 4 - rel, 4) * PART + c * WIDE, WIDE)
                term = dot(normed, wqkv[pl.ds(at, WIDE), :])
                result = term if result is None else result + term
        query = turned(result[:, :HS])
        key = turned(result[:, HS : 2 * HS])
        kv = jnp.concatenate([key, result[:, 2 * HS :].astype(BF16)], axis=1)
        kv_own[m] = kv
        kv_in[m, 0] = kv
        for o in range(1, EXPERTS):
            msg.send(kv_own.at[m], kv_in.at[m, o], kv_leave[m], kv_come[m], expert=peer[o])
        return query

    def attend(m, query):
        column = lax.broadcasted_iota(jnp.int32, (ROWS, LENGTH), 1)
        source = e - column // ROWS
        source = jnp.where(source < 0, source + EXPERTS, source)
        row = e * ROWS + lax.broadcasted_iota(jnp.int32, (ROWS, LENGTH), 0)
        causal = source * ROWS + column % ROWS <= row
        msg.wait(kv_come[m])
        kv = kv_in[m].reshape(LENGTH, 2 * HS)
        scores = lax.dot_general(
            query, kv[:, :HS], (((1,), (1,)), ((), ())), preferred_element_type=F32
        )
        scores = jnp.where(causal, scores * HS ** (-0.5), NEGATIVE)
        highest = jnp.max(scores, axis=-1, keepdims=True)
        weights = jnp.where(causal, jnp.exp(scores - highest), 0.0)
        total = jnp.sum(weights, axis=-1, keepdims=True)
        context[m] = (dot(weights.astype(BF16), kv[:, HS:]) / total).astype(BF16)

    def split_weights():
        step = 512
        row = lax.broadcasted_iota(jnp.int32, (step // 2, step), 0)
        col = lax.broadcasted_iota(jnp.int32, (step // 2, step), 1)

        def body(i, _):
            block = wkv[pl.ds(pl.multiple_of(i * step, step), step), :]
            to = pl.ds(pl.multiple_of(i * (step // 2), step // 2), step // 2)
            for k in range(2):
                pick = jnp.where(col == 2 * row + k, 1.0, 0.0).astype(BF16)
                wqkv[to, (k + 1) * HS : (k + 2) * HS] = dot(pick, block).astype(BF16)
            return 0

        lax.fori_loop(0, wkv.shape[0] // step, body, 0)

    place_rows(0)
    dispatch(0)
    gather_send(0, [0])
    place_rows(1)
    gather_send(0, [1, 2, 3, 4])
    dispatch(1)
    gather_send(0, [5, 6, 7])
    gains_come = to_tensor_peers(gains)
    for load in loads[5:]:
        load.wait()
    expert_in(0, 0)
    gather_forward(0)
    gather_send(1, range(EXPERTS))
    split_weights()
    msg.wait(x_come_r[0][near])
    expert_in(0, RIGHT)
    msg.wait(x_come_l[0][0])
    expert_in(0, LEFT)
    msg.wait(ahead_come_r[0])
    msg.wait(ahead_come_l[0])
    expert_in(0, OPPOSITE)
    activate(0)
    for c in range(CUTS):
        send_opposite(0, c)
        send_direct(0, c)
    for c in range(CUTS):
        own[0, c] = part(0, c, 0)
    expert_in(1, 0)
    gather_forward(1)
    for c in range(CUTS):
        sum_middle(0, c)
    msg.wait(x_come_r[1][near])
    expert_in(1, RIGHT)
    msg.wait(x_come_l[1][0])
    expert_in(1, LEFT)
    msg.wait(ahead_come_r[1])
    msg.wait(ahead_come_l[1])
    expert_in(1, OPPOSITE)
    activate(1)
    send_opposite(1, 0)
    send_direct(1, 0)
    send_opposite(1, 1)
    sum_last(0, 0)
    sum_middle(1, 0)
    send_direct(1, 1)
    sum_last(0, 1)
    for c in range(CUTS):
        own[1, c] = part(1, c, 0)
    sum_middle(1, 1)
    combine(0, 0)
    combine(0, 1)
    sum_last(1, 0)
    rows_send(0, 0)
    rows_send(0, 1)
    sum_last(1, 1)
    msg.wait(gains_come)
    rows_forward(0, 0)
    rows_forward(0, 1)
    combine(1, 0)
    query0 = project(0)
    combine(1, 1)
    rows_send(1, 0)
    rows_send(1, 1)
    attend(0, query0)
    rows_forward(1, 0)
    rows_forward(1, 1)
    query1 = project(1)
    attend(1, query1)

    writes = [
        pltpu.make_async_copy(context, context_out, local_sems.at[len(loads) + len(moe_writes)])
    ]
    writes[0].start()
    for write in writes + moe_writes:
        write.wait()
    msg.finish()


def per_device(
    stream, expert_ids, expert_gates, moe_gain, w_gate, w_up, w_down, attn_gain, w_query, w_keyval
):
    hbm = pl.BlockSpec(memory_space=pl.ANY)
    slots_cut = (MICRO, CUTS, SLOTS, WIDE)
    half_cut = (MICRO, CUTS, HALF, WIDE)
    scratch = [
        ((MICRO, ROWS, PART), BF16),
        ((MICRO, 2, ROWS), jnp.int32),
        ((MICRO, 2, ROWS), F32),
        ((1, PART), BF16),
        ((1, PART), BF16),
        ((4 * PART, 2 * FF), BF16),
        ((FF, 4 * PART), BF16),
        ((4 * PART, 3 * HS), BF16),
        ((8 * PART, HS), BF16),
        ((ROWS, 2 * HS), F32),
        ((4, 8, MICRO * ROWS), F32),
        ((4, 16, PART), BF16),
        ((MICRO, EXPERTS, CAP, PART), BF16),
        ((MICRO, 4, EXPERTS, CAP, PART), BF16),
        ((SLOTS, 2 * FF), F32),
        ((MICRO, SLOTS, FF), BF16),
        (slots_cut, I16),
        (slots_cut, I16),
        (slots_cut, I16),
        (half_cut, F32),
        (half_cut, F32),
        (slots_cut, F32),
        (half_cut, I16),
        (half_cut, I16),
        (slots_cut, I16),
        (slots_cut, I16),
    ]
    scratch += [((MICRO, CUTS, 8, HALF), F32)] * 8
    scratch += [
        ((MICRO, CUTS, EXPERTS, CAP, WIDE), BF16),
        ((MICRO, CUTS, EXPERTS, CAP, WIDE), BF16),
        ((MICRO, CUTS, ROWS, WIDE), BF16),
        ((MICRO, 4, CUTS, ROWS, WIDE), BF16),
        ((MICRO, ROWS, 2 * HS), BF16),
        ((MICRO, EXPERTS, ROWS, 2 * HS), BF16),
        ((MICRO, ROWS, HS), BF16),
    ]
    moe, context = pl.pallas_call(
        kernel,
        out_shape=(
            jax.ShapeDtypeStruct((MICRO, ROWS, PART), BF16),
            jax.ShapeDtypeStruct((MICRO, ROWS, HS), BF16),
        ),
        in_specs=[hbm] * 11,
        out_specs=(hbm, hbm),
        scratch_shapes=[pltpu.VMEM(shape, kind) for shape, kind in scratch]
        + [pltpu.SemaphoreType.DMA((16,)), pltpu.SemaphoreType.DMA((SEMAPHORES,))],
        compiler_params=pltpu.CompilerParams(
            collective_id=0, has_side_effects=True, vmem_limit_bytes=56 * 1024 * 1024
        ),
        cost_estimate=pl.CostEstimate(
            flops=5_300_000_000, bytes_accessed=13_000_000, transcendentals=500_000
        ),
    )(
        stream[0],
        jnp.transpose(expert_ids[0], (0, 2, 1)),
        jnp.transpose(expert_gates[0], (0, 2, 1)),
        moe_gain,
        attn_gain,
        w_gate[0, 0],
        w_up[0, 0],
        w_down[0, 0],
        w_query[0],
        w_keyval[0].reshape(8 * PART, HS),
        jnp.asarray(rope_table(LENGTH)),
    )
    return moe[None], context[None]


def solution(mesh):
    placed = (
        P("pipe", None, "expert", "tensor"),
        P("pipe", None, "expert", None),
        P("pipe", None, "expert", None),
        P("pipe", "tensor"),
        P("pipe", "expert", None, "tensor"),
        P("pipe", "expert", None, "tensor"),
        P("pipe", "expert", "tensor", None),
        P("pipe", "tensor"),
        P("pipe", None, "tensor"),
        P("pipe", None, None, "tensor"),
    )
    return jax.shard_map(
        per_device,
        mesh=mesh,
        in_specs=placed,
        out_specs=(P("pipe", None, "expert", "tensor"), P("pipe", None, "expert", "tensor")),
        check_vma=False,
    )
```

```python
import jax
import jax.numpy as jnp
import numpy as np
from jax import lax
from jax.experimental import pallas as pl
from jax.experimental.pallas import tpu as pltpu
from jax.sharding import PartitionSpec as P

MESH = pl.DeviceIdType.MESH
HS = 128
EPS = 1e-05
THETA = 1000000.0
NEGATIVE = -1e30
F32 = jnp.float32
BF16 = jnp.bfloat16
I16 = jnp.int16

MICRO = 2
ROWS = 64
PART = 1024
CAP = 32
EXPERTS = 8
SLOTS = EXPERTS * CAP
HALF = SLOTS // 2
CUTS = 2
WIDE = PART // CUTS
SHARE = 384
KEEP = PART - SHARE
FF = 384
LENGTH = EXPERTS * ROWS
RIGHT, OPPOSITE, LEFT = 1, 2, 3
SEMAPHORES = 136


def rope_table(length):
    freqs = THETA ** (-2.0 * np.arange(HS // 2) / HS)
    angles = np.arange(length)[:, None] * freqs[None, :]
    cosine, sine = np.cos(angles), np.sin(angles)
    return np.concatenate([cosine, cosine, -sine, sine], axis=1).astype(np.float32)


class Group:
    def __init__(self, sem, whole):
        self.sem, self.whole, self.sent, self.waited = sem, whole, False, False


class Messages:
    def __init__(self, sems):
        self.sems, self.used, self.sends, self.recvs = sems, 0, [], []

    def group(self, whole, kind):
        found = Group(self.sems.at[self.used], whole)
        self.used += 1
        kind.append(found)
        return found

    def leaving(self, whole):
        return self.group(whole, self.sends)

    def coming(self, whole):
        return self.group(whole, self.recvs)

    def send(self, src, dst, leaving, coming, **where):
        pltpu.make_async_remote_copy(
            src_ref=src,
            dst_ref=dst,
            send_sem=leaving.sem,
            recv_sem=coming.sem,
            device_id=where,
            device_id_type=MESH,
        ).start()
        leaving.sent = coming.sent = True

    def _any(self, found):
        return pltpu.make_async_remote_copy(
            src_ref=found.whole,
            dst_ref=found.whole,
            send_sem=found.sem,
            recv_sem=found.sem,
            device_id={"tensor": lax.rem(lax.axis_index("tensor") + 1, 4)},
            device_id_type=MESH,
        )

    def wait(self, found):
        self._any(found).wait_recv()
        found.waited = True

    def finish(self):
        for found in self.recvs:
            if found.sent and not found.waited:
                self.wait(found)
        for found in self.sends:
            if found.sent:
                self._any(found).wait_send()


def dot(a, b):
    return jnp.dot(a, b, preferred_element_type=F32)


def dot_first(a, b):
    return lax.dot_general(a, b, (((0,), (0,)), ((), ())), preferred_element_type=F32)


def flipped(line):
    n = max(line.shape)
    diagonal = lax.broadcasted_iota(jnp.int32, (n, n), 0) == lax.broadcasted_iota(
        jnp.int32, (n, n), 1
    )
    axis = 0 if line.shape[1] == 1 else 1
    return jnp.sum(jnp.where(diagonal, line, 0.0), axis=axis, keepdims=True)


def encoded(value):
    highest = jnp.maximum(jnp.max(jnp.abs(value), axis=1, keepdims=True), 1e-30)
    codes = jnp.round(value * (32760.0 / highest)).astype(jnp.int32).astype(I16)
    return codes, highest * (1.0 / 32760.0)


def decoded(codes, step):
    return codes.astype(jnp.int32).astype(F32) * step


def kernel(
    stream_hbm, ids_hbm, gates_hbm, mgain_hbm, again_hbm,
    wg_hbm, wu_hbm, wd_hbm, wq_hbm, wkv_hbm, rope_hbm,
    moe_out, context_out,
    stream, ids, gates, mgain, again, w13, wd, wqkv, wkv, rope,
    ssq, gains, raw, out, x, out_all, x_all, rates_out, rates_in, acc, hidden,
    opp, going_r, going_l, part_r, part_l, own, opp_l, opp_r, sum_l, sum_r,
    steps_r, steps_l, steps_from_r, steps_from_l, more_r, more_l, more_from_r, more_from_l,
    eo, ret, mixed, rows_in, kv_own, kv_in, context,
    local_sems, sems,
):
    e, t, p = lax.axis_index("expert"), lax.axis_index("tensor"), lax.axis_index("pipe")
    right, left, opposite = lax.rem(t + 1, 4), lax.rem(t + 3, 4), lax.rem(t + 2, 4)
    after, before = lax.rem(p + 1, 8), lax.rem(p + 7, 8)
    peer = [lax.rem(e + o, EXPERTS) for o in range(EXPERTS)]
    msg = Messages(sems)

    here = pl.ds(pl.multiple_of(e * ROWS, ROWS), ROWS)
    loads = [
        (stream_hbm, stream),
        (ids_hbm, ids),
        (mgain_hbm, mgain),
        (gates_hbm, gates),
        (again_hbm, again),
        (wg_hbm, w13.at[:, :FF]),
        (wu_hbm, w13.at[:, FF:]),
        (wd_hbm, wd),
        (wq_hbm, wqkv.at[:, :HS]),
        (wkv_hbm, wkv),
        (rope_hbm.at[here], rope),
    ]
    loads = [pltpu.make_async_copy(s, d, local_sems.at[i]) for i, (s, d) in enumerate(loads)]
    for load in loads:
        load.start()

    barrier = pltpu.get_barrier_semaphore()
    peers = [{"expert": other} for other in peer[1:]]
    peers += [{"tensor": other} for other in (right, left, opposite)]
    peers += [{"pipe": other} for other in (after, before)]
    for other in peers:
        pl.semaphore_signal(barrier, inc=1, device_id=other, device_id_type=MESH)

    slot = lax.broadcasted_iota(jnp.int32, (SLOTS, ROWS), 0)
    group, place = slot // CAP, slot % CAP
    expert_of = jnp.where(group + e >= EXPERTS, group + e - EXPERTS, group + e)
    row_of = lax.broadcasted_iota(jnp.int32, (ROWS, ROWS), 0)
    col_of = lax.broadcasted_iota(jnp.int32, (ROWS, ROWS), 1)
    earlier = jnp.where(row_of < col_of, 1.0, 0.0).astype(BF16)
    for load in loads[:5]:
        load.wait()
    chosen = []
    for m in range(MICRO):
        first = ids[m, 0:1, :] == expert_of
        second = ids[m, 1:2, :] == expert_of
        named = jnp.where(first | second, 1.0, 0.0)
        taken = dot(named.astype(BF16), earlier) == place.astype(F32)
        chosen.append(
            [jnp.where(which & taken, 1.0, 0.0).astype(BF16) for which in (first, second)]
        )

    value = stream[...].reshape(MICRO * ROWS, PART).astype(F32)
    ssq[0] = jnp.broadcast_to(flipped(jnp.sum(value * value, axis=1, keepdims=True)), (8, MICRO * ROWS))
    gains[0, :8] = jnp.broadcast_to(mgain[...], (8, PART))
    gains[0, 8:] = jnp.broadcast_to(again[...], (8, PART))
    raw[0] = stream[:, :, KEEP:]

    pl.semaphore_wait(barrier, len(peers))

    def to_tensor_peers(buffer):
        leaving, coming = msg.leaving(buffer.at[1:4]), msg.coming(buffer.at[1:4])
        for rel, other in ((RIGHT, right), (LEFT, left), (OPPOSITE, opposite)):
            msg.send(buffer.at[0], buffer.at[rel], leaving, coming, tensor=other)
        return coming

    out_leave = [msg.leaving(out.at[m, 1:]) for m in range(MICRO)]
    out_come = [[None] + [msg.coming(x.at[m, 0, o]) for o in range(1, EXPERTS)] for m in range(MICRO)]
    all_leave = [msg.leaving(out_all.at[m, 1:]) for m in range(MICRO)]
    all_come = [msg.coming(x_all.at[m, 1:]) for m in range(MICRO)]
    rates_leave, rates_come = msg.leaving(rates_out.at[1:]), msg.coming(rates_in.at[1:])
    x_leave_r = [msg.leaving(x.at[m, 0]) for m in range(MICRO)]
    x_leave_l = [msg.leaving(x.at[m, 0]) for m in range(MICRO)]
    near = EXPERTS // 2
    x_come_r = [
        [msg.coming(x.at[m, RIGHT, o]) for o in range(near)] + [msg.coming(x.at[m, RIGHT, near:])] * near
        for m in range(MICRO)
    ]
    x_come_l = [
        [msg.coming(x.at[m, LEFT, :near])] * near + [msg.coming(x.at[m, LEFT, o]) for o in range(near, EXPERTS)]
        for m in range(MICRO)
    ]
    ahead_leave_r = [msg.leaving(x.at[m, RIGHT, :near]) for m in range(MICRO)]
    ahead_leave_l = [msg.leaving(x.at[m, LEFT, near:]) for m in range(MICRO)]
    ahead_come_r = [msg.coming(x.at[m, OPPOSITE, :near]) for m in range(MICRO)]
    ahead_come_l = [msg.coming(x.at[m, OPPOSITE, near:]) for m in range(MICRO)]

    placing = [chosen[m][0] + chosen[m][1] for m in range(MICRO)]

    def dispatch(m):
        block = dot(placing[m], stream[m, :, :KEEP]).astype(BF16).reshape(EXPERTS, CAP, KEEP)
        x[m, 0, 0] = block[0]
        out[m] = block
        for o in range(1, EXPERTS):
            msg.send(out.at[m, o], x.at[m, 0, o], out_leave[m], out_come[m][o], expert=peer[o])

    def dispatch_all(m):
        for rel in range(4):
            at = slice(rel * SHARE, (rel + 1) * SHARE)
            block = dot(placing[m], raw[rel, m]).astype(BF16).reshape(EXPERTS, CAP, SHARE)
            x_all[m, 0, :, at] = block[0]
            out_all[m, :, :, at] = block
        for o in range(1, EXPERTS):
            msg.send(out_all.at[m, o], x_all.at[m, o], all_leave[m], all_come[m], expert=peer[o])

    def dispatch_rates():
        total = (ssq[0, 0:1, :] + ssq[1, 0:1, :]) + (ssq[2, 0:1, :] + ssq[3, 0:1, :])
        scales = lax.rsqrt(total * (1.0 / (4 * PART)) + EPS)
        rates_out[...] = jnp.zeros(rates_out.shape, F32)
        for m in range(MICRO):
            scale = scales[:, m * ROWS : (m + 1) * ROWS]
            rate = jnp.sum(placing[m].astype(F32) * scale, axis=1, keepdims=True)
            for o in range(EXPERTS):
                rates_out[o, m : m + 1, :CAP] = flipped(rate[o * CAP : (o + 1) * CAP])
        rates_in[0] = rates_out[0]
        for o in range(1, EXPERTS):
            msg.send(rates_out.at[o], rates_in.at[o], rates_leave, rates_come, expert=peer[o])

    def rates_of(m):
        return jnp.concatenate(
            [flipped(rates_in[o, m : m + 1, :CAP]) for o in range(EXPERTS)], axis=0
        )

    def gather_send(m, pieces):
        for o in pieces:
            if o > 0:
                msg.wait(out_come[m][o])
            msg.send(x.at[m, 0, o], x.at[m, RIGHT, o], x_leave_r[m], x_come_r[m][o], tensor=right)
            msg.send(x.at[m, 0, o], x.at[m, LEFT, o], x_leave_l[m], x_come_l[m][o], tensor=left)

    def gather_forward(m):
        for i in range(near):
            msg.wait(x_come_r[m][i])
            msg.send(x.at[m, RIGHT, i], x.at[m, OPPOSITE, i], ahead_leave_r[m], ahead_come_r[m], tensor=right)
            o = i + near
            msg.wait(x_come_l[m][o])
            msg.send(x.at[m, LEFT, o], x.at[m, OPPOSITE, o], ahead_leave_l[m], ahead_come_l[m], tensor=left)

    def columns_of(rel, first, width):
        return pl.ds(pl.multiple_of(lax.rem(t + 4 - rel, 4) * PART + first, HS), width)

    def normed_rows(rows, rate, gain):
        return (rows.astype(F32) * rate * gain.astype(F32)).astype(BF16)

    def expert_in(m, rel):
        rows = x[m, rel].reshape(SLOTS, KEEP)
        normed = normed_rows(rows, rates_of(m), gains[rel, 0:1, :KEEP])
        value = dot(normed, w13[columns_of(rel, 0, KEEP), :])
        acc[...] = value if rel == 0 else acc[...] + value

    def expert_in_all(m):
        value = None
        for rel in range(4):
            rows = x_all[m, :, :, rel * SHARE : (rel + 1) * SHARE].reshape(SLOTS, SHARE)
            normed = normed_rows(rows, rates_of(m), gains[rel, 0:1, KEEP:])
            term = dot(normed, w13[columns_of(rel, KEEP, SHARE), :])
            value = term if value is None else value + term
        acc[...] += value

    def activate(m):
        gated, lifted = acc[:, :FF], acc[:, FF:]
        hidden[m] = (gated / (1.0 + jnp.exp(-gated)) * lifted).astype(BF16)

    def pairs(buffer, kind):
        return [kind(buffer.at[m]) for m in range(MICRO)]

    def each(buffer, rows):
        return [[msg.coming(buffer.at[m, c, rows]) for c in range(CUTS)] for m in range(MICRO)]

    top, low, every = slice(0, HALF), slice(HALF, SLOTS), slice(None)
    opp_leave, going_r_leave, going_l_leave = (
        pairs(b, msg.leaving) for b in (opp, going_r, going_l)
    )
    steps_r_leave, steps_l_leave, more_r_leave, more_l_leave = (
        pairs(b, msg.leaving) for b in (steps_r, steps_l, more_r, more_l)
    )
    opp_l_come, opp_r_come = each(opp_l, every), each(opp_r, every)
    sum_l_top, sum_l_low = each(sum_l, top), each(sum_l, low)
    sum_r_top, sum_r_low = each(sum_r, top), each(sum_r, low)
    steps_l_come, steps_r_come = each(steps_from_l, every), each(steps_from_r, every)
    more_l_come, more_r_come = each(more_from_l, every), each(more_from_r, every)

    def part(m, c, rel):
        at = pl.multiple_of(lax.rem(t + rel, 4) * PART + c * WIDE, WIDE)
        return dot(hidden[m], wd[:, pl.ds(at, WIDE)])

    def send_opposite(m, c):
        opp[m, c], step = encoded(part(m, c, OPPOSITE))
        for ref in (steps_r, steps_l, more_r, more_l):
            ref[m, c] = jnp.zeros((8, HALF), F32)
        steps_r[m, c, 0:1] = flipped(step[:HALF])
        steps_l[m, c, 0:1] = flipped(step[HALF:])
        msg.send(opp.at[m, c, top], opp_l.at[m, c], opp_leave[m], opp_l_come[m][c], tensor=right)
        msg.send(opp.at[m, c, low], opp_r.at[m, c], opp_leave[m], opp_r_come[m][c], tensor=left)

    def send_direct(m, c):
        value = part(m, c, RIGHT)
        part_r[m, c] = value[:HALF]
        going_r[m, c, low], step = encoded(value[HALF:])
        steps_r[m, c, 1:2] = flipped(step)
        msg.send(steps_r.at[m, c], steps_from_l.at[m, c], steps_r_leave[m], steps_l_come[m][c], tensor=right)
        msg.send(going_r.at[m, c, low], sum_l.at[m, c, low], going_r_leave[m], sum_l_low[m][c], tensor=right)
        value = part(m, c, LEFT)
        part_l[m, c] = value[HALF:]
        going_l[m, c, top], step = encoded(value[:HALF])
        steps_l[m, c, 1:2] = flipped(step)
        msg.send(steps_l.at[m, c], steps_from_r.at[m, c], steps_l_leave[m], steps_r_come[m][c], tensor=left)
        msg.send(going_l.at[m, c, top], sum_r.at[m, c, top], going_l_leave[m], sum_r_top[m][c], tensor=left)

    def sum_middle(m, c):
        msg.wait(steps_l_come[m][c])
        msg.wait(opp_l_come[m][c])
        value = part_r[m, c] + decoded(opp_l[m, c], flipped(steps_from_l[m, c, 0:1]))
        going_r[m, c, top], step = encoded(value)
        more_r[m, c, 0:1] = flipped(step)
        msg.send(more_r.at[m, c], more_from_l.at[m, c], more_r_leave[m], more_l_come[m][c], tensor=right)
        msg.send(going_r.at[m, c, top], sum_l.at[m, c, top], going_r_leave[m], sum_l_top[m][c], tensor=right)
        msg.wait(steps_r_come[m][c])
        msg.wait(opp_r_come[m][c])
        value = part_l[m, c] + decoded(opp_r[m, c], flipped(steps_from_r[m, c, 0:1]))
        going_l[m, c, low], step = encoded(value)
        more_l[m, c, 0:1] = flipped(step)
        msg.send(more_l.at[m, c], more_from_r.at[m, c], more_l_leave[m], more_r_come[m][c], tensor=left)
        msg.send(going_l.at[m, c, low], sum_r.at[m, c, low], going_l_leave[m], sum_r_low[m][c], tensor=left)

    eo_leave = [msg.leaving(eo.at[m, :, 1:]) for m in range(MICRO)]
    ret_come = [[msg.coming(ret.at[m, c, 1:]) for c in range(CUTS)] for m in range(MICRO)]

    def sum_last(m, c):
        for found in (sum_l_low, sum_r_top, more_l_come, sum_l_top, more_r_come, sum_r_low):
            msg.wait(found[m][c])
        above = own[m, c, top] + (
            decoded(sum_l[m, c, top], flipped(more_from_l[m, c, 0:1]))
            + decoded(sum_r[m, c, top], flipped(steps_from_r[m, c, 1:2]))
        )
        below = own[m, c, low] + (
            decoded(sum_l[m, c, low], flipped(steps_from_l[m, c, 1:2]))
            + decoded(sum_r[m, c, low], flipped(more_from_r[m, c, 0:1]))
        )
        value = jnp.concatenate([above.astype(BF16), below.astype(BF16)], axis=0)
        value = value.reshape(EXPERTS, CAP, WIDE)
        ret[m, c, 0] = value[0]
        eo[m, c] = value
        for o in range(1, EXPERTS):
            msg.send(
                eo.at[m, c, o], ret.at[m, c, o], eo_leave[m], ret_come[m][c],
                expert=lax.rem(e + EXPERTS - o, EXPERTS),
            )

    mixed_leave = [msg.leaving(mixed.at[m]) for m in range(MICRO)]
    moe_writes = []
    shift_come = [[msg.coming(rows_in.at[m, 0, c]) for c in range(CUTS)] for m in range(MICRO)]

    def combine(m, c):
        msg.wait(ret_come[m][c])
        returned = ret[m, c].reshape(SLOTS, WIDE)
        columns = slice(c * WIDE, (c + 1) * WIDE)
        value = None
        for k in range(2):
            term = flipped(gates[m, k : k + 1, :]) * dot_first(chosen[m][k], returned)
            value = term if value is None else value + term
        mixed[m, c] = (stream[m, :, columns].astype(F32) + value).astype(BF16)
        msg.send(mixed.at[m, c], rows_in.at[m, 0, c], mixed_leave[m], shift_come[m][c], pipe=after)
        number = len(loads) + len(moe_writes)
        moe_writes.append(
            pltpu.make_async_copy(mixed.at[m, c], moe_out.at[m, :, columns], local_sems.at[number])
        )
        moe_writes[-1].start()

    rows_leave = [msg.leaving(rows_in.at[m, 1:]) for m in range(MICRO)]
    rows_come = [[msg.coming(rows_in.at[m, 1:, c]) for c in range(CUTS)] for m in range(MICRO)]

    def rows_send(m, c):
        msg.wait(shift_come[m][c])
        for rel, other in ((OPPOSITE, opposite), (RIGHT, right), (LEFT, left)):
            msg.send(
                rows_in.at[m, 0, c], rows_in.at[m, rel, c], rows_leave[m], rows_come[m][c], tensor=other
            )

    kv_leave = [msg.leaving(kv_in.at[m, 1:]) for m in range(MICRO)]
    kv_come = [msg.coming(kv_in.at[m, 1:]) for m in range(MICRO)]

    def turned(value):
        swapped = pltpu.roll(value, HS // 2, 1)
        return (value * rope[:, :HS] + swapped * rope[:, HS:]).astype(BF16)

    def project(m):
        for c in range(CUTS):
            msg.wait(rows_come[m][c])
        total = None
        for rel in range(4):
            for c in range(CUTS):
                value = rows_in[m, rel, c].astype(F32)
                term = jnp.sum(value * value, axis=-1, keepdims=True)
                total = term if total is None else total + term
        scale = lax.rsqrt(total * (1.0 / (4 * PART)) + EPS)
        result = None
        for rel in range(4):
            for c in range(CUTS):
                gain = gains[rel, 8:9, c * WIDE : (c + 1) * WIDE].astype(F32)
                normed = (rows_in[m, rel, c].astype(F32) * scale * gain).astype(BF16)
                at = pl.multiple_of(lax.rem(t + 4 - rel, 4) * PART + c * WIDE, WIDE)
                term = dot(normed, wqkv[pl.ds(at, WIDE), :])
                result = term if result is None else result + term
        query = turned(result[:, :HS])
        key = turned(result[:, HS : 2 * HS])
        kv = jnp.concatenate([key, result[:, 2 * HS :].astype(BF16)], axis=1)
        kv_own[m] = kv
        kv_in[m, 0] = kv
        for o in range(1, EXPERTS):
            msg.send(kv_own.at[m], kv_in.at[m, o], kv_leave[m], kv_come[m], expert=peer[o])
        return query

    def attend(m, query):
        column = lax.broadcasted_iota(jnp.int32, (ROWS, LENGTH), 1)
        source = e - column // ROWS
        source = jnp.where(source < 0, source + EXPERTS, source)
        row = e * ROWS + lax.broadcasted_iota(jnp.int32, (ROWS, LENGTH), 0)
        causal = source * ROWS + column % ROWS <= row
        msg.wait(kv_come[m])
        kv = kv_in[m].reshape(LENGTH, 2 * HS)
        scores = lax.dot_general(
            query, kv[:, :HS], (((1,), (1,)), ((), ())), preferred_element_type=F32
        )
        scores = jnp.where(causal, scores * HS ** (-0.5), NEGATIVE)
        highest = jnp.max(scores, axis=-1, keepdims=True)
        weights = jnp.where(causal, jnp.exp(scores - highest), 0.0)
        total = jnp.sum(weights, axis=-1, keepdims=True)
        context[m] = (dot(weights.astype(BF16), kv[:, HS:]) / total).astype(BF16)

    def split_weights():
        step = 512
        row = lax.broadcasted_iota(jnp.int32, (step // 2, step), 0)
        col = lax.broadcasted_iota(jnp.int32, (step // 2, step), 1)

        def body(i, _):
            block = wkv[pl.ds(pl.multiple_of(i * step, step), step), :]
            to = pl.ds(pl.multiple_of(i * (step // 2), step // 2), step // 2)
            for k in range(2):
                pick = jnp.where(col == 2 * row + k, 1.0, 0.0).astype(BF16)
                wqkv[to, (k + 1) * HS : (k + 2) * HS] = dot(pick, block).astype(BF16)
            return 0

        lax.fori_loop(0, wkv.shape[0] // step, body, 0)

    raw_come = to_tensor_peers(raw)
    dispatch(0)
    ssq_come = to_tensor_peers(ssq)
    gather_send(0, [0])
    gains_come = to_tensor_peers(gains)
    dispatch(1)
    msg.wait(ssq_come)
    dispatch_rates()
    gather_send(0, [1, 2, 3])
    msg.wait(raw_come)
    dispatch_all(0)
    gather_send(0, [4, 5, 6, 7])
    dispatch_all(1)
    for load in loads[5:]:
        load.wait()
    msg.wait(rates_come)
    msg.wait(gains_come)
    expert_in(0, 0)
    gather_forward(0)
    gather_send(1, range(EXPERTS))
    split_weights()
    msg.wait(x_come_r[0][near])
    expert_in(0, RIGHT)
    msg.wait(x_come_l[0][0])
    expert_in(0, LEFT)
    msg.wait(ahead_come_r[0])
    msg.wait(ahead_come_l[0])
    expert_in(0, OPPOSITE)
    msg.wait(all_come[0])
    expert_in_all(0)
    activate(0)
    for c in range(CUTS):
        send_opposite(0, c)
        send_direct(0, c)
    for c in range(CUTS):
        own[0, c] = part(0, c, 0)
    expert_in(1, 0)
    gather_forward(1)
    for c in range(CUTS):
        sum_middle(0, c)
    msg.wait(x_come_r[1][near])
    expert_in(1, RIGHT)
    msg.wait(x_come_l[1][0])
    expert_in(1, LEFT)
    msg.wait(ahead_come_r[1])
    msg.wait(ahead_come_l[1])
    expert_in(1, OPPOSITE)
    msg.wait(all_come[1])
    expert_in_all(1)
    activate(1)
    send_opposite(1, 0)
    send_direct(1, 0)
    send_opposite(1, 1)
    sum_last(0, 0)
    sum_middle(1, 0)
    send_direct(1, 1)
    sum_last(0, 1)
    for c in range(CUTS):
        own[1, c] = part(1, c, 0)
    sum_middle(1, 1)
    combine(0, 0)
    combine(0, 1)
    sum_last(1, 0)
    rows_send(0, 0)
    rows_send(0, 1)
    sum_last(1, 1)
    combine(1, 0)
    query0 = project(0)
    combine(1, 1)
    rows_send(1, 0)
    rows_send(1, 1)
    attend(0, query0)
    query1 = project(1)
    attend(1, query1)

    writes = [
        pltpu.make_async_copy(context, context_out, local_sems.at[len(loads) + len(moe_writes)])
    ]
    writes[0].start()
    for write in writes + moe_writes:
        write.wait()
    msg.finish()


def per_device(
    stream, expert_ids, expert_gates, moe_gain, w_gate, w_up, w_down, attn_gain, w_query, w_keyval
):
    hbm = pl.BlockSpec(memory_space=pl.ANY)
    slots_cut = (MICRO, CUTS, SLOTS, WIDE)
    half_cut = (MICRO, CUTS, HALF, WIDE)
    scratch = [
        ((MICRO, ROWS, PART), BF16),
        ((MICRO, 2, ROWS), jnp.int32),
        ((MICRO, 2, ROWS), F32),
        ((1, PART), BF16),
        ((1, PART), BF16),
        ((4 * PART, 2 * FF), BF16),
        ((FF, 4 * PART), BF16),
        ((4 * PART, 3 * HS), BF16),
        ((8 * PART, HS), BF16),
        ((ROWS, 2 * HS), F32),
        ((4, 8, MICRO * ROWS), F32),
        ((4, 16, PART), BF16),
        ((4, MICRO, ROWS, SHARE), BF16),
        ((MICRO, EXPERTS, CAP, KEEP), BF16),
        ((MICRO, 4, EXPERTS, CAP, KEEP), BF16),
        ((MICRO, EXPERTS, CAP, 4 * SHARE), BF16),
        ((MICRO, EXPERTS, CAP, 4 * SHARE), BF16),
        ((EXPERTS, 8, HS), F32),
        ((EXPERTS, 8, HS), F32),
        ((SLOTS, 2 * FF), F32),
        ((MICRO, SLOTS, FF), BF16),
        (slots_cut, I16),
        (slots_cut, I16),
        (slots_cut, I16),
        (half_cut, F32),
        (half_cut, F32),
        (slots_cut, F32),
        (half_cut, I16),
        (half_cut, I16),
        (slots_cut, I16),
        (slots_cut, I16),
    ]
    scratch += [((MICRO, CUTS, 8, HALF), F32)] * 8
    scratch += [
        ((MICRO, CUTS, EXPERTS, CAP, WIDE), BF16),
        ((MICRO, CUTS, EXPERTS, CAP, WIDE), BF16),
        ((MICRO, CUTS, ROWS, WIDE), BF16),
        ((MICRO, 4, CUTS, ROWS, WIDE), BF16),
        ((MICRO, ROWS, 2 * HS), BF16),
        ((MICRO, EXPERTS, ROWS, 2 * HS), BF16),
        ((MICRO, ROWS, HS), BF16),
    ]
    moe, context = pl.pallas_call(
        kernel,
        out_shape=(
            jax.ShapeDtypeStruct((MICRO, ROWS, PART), BF16),
            jax.ShapeDtypeStruct((MICRO, ROWS, HS), BF16),
        ),
        in_specs=[hbm] * 11,
        out_specs=(hbm, hbm),
        scratch_shapes=[pltpu.VMEM(shape, kind) for shape, kind in scratch]
        + [pltpu.SemaphoreType.DMA((16,)), pltpu.SemaphoreType.DMA((SEMAPHORES,))],
        compiler_params=pltpu.CompilerParams(
            collective_id=0, has_side_effects=True, vmem_limit_bytes=56 * 1024 * 1024
        ),
        cost_estimate=pl.CostEstimate(
            flops=5_300_000_000, bytes_accessed=13_000_000, transcendentals=500_000
        ),
    )(
        stream[0],
        jnp.transpose(expert_ids[0], (0, 2, 1)),
        jnp.transpose(expert_gates[0], (0, 2, 1)),
        moe_gain,
        attn_gain,
        w_gate[0, 0],
        w_up[0, 0],
        w_down[0, 0],
        w_query[0],
        w_keyval[0].reshape(8 * PART, HS),
        jnp.asarray(rope_table(LENGTH)),
    )
    return moe[None], context[None]


def solution(mesh):
    placed = (
        P("pipe", None, "expert", "tensor"),
        P("pipe", None, "expert", None),
        P("pipe", None, "expert", None),
        P("pipe", "tensor"),
        P("pipe", "expert", None, "tensor"),
        P("pipe", "expert", None, "tensor"),
        P("pipe", "expert", "tensor", None),
        P("pipe", "tensor"),
        P("pipe", None, "tensor"),
        P("pipe", None, None, "tensor"),
    )
    return jax.shard_map(
        per_device,
        mesh=mesh,
        in_specs=placed,
        out_specs=(P("pipe", None, "expert", "tensor"), P("pipe", None, "expert", "tensor")),
        check_vma=False,
    )
```

```python
import jax
import jax.numpy as jnp
import numpy as np
from jax import lax
from jax.experimental import pallas as pl
from jax.experimental.pallas import tpu as pltpu
from jax.sharding import PartitionSpec as P

MESH = pl.DeviceIdType.MESH
HS = 128
EPS = 1e-05
THETA = 1000000.0
NEGATIVE = -1e30
F32 = jnp.float32
BF16 = jnp.bfloat16
I16 = jnp.int16

MICRO = 2
ROWS = 64
PART = 1024
CAP = 32
EXPERTS = 8
SLOTS = EXPERTS * CAP
HALF = SLOTS // 2
CUTS = 2
WIDE = PART // CUTS
SHARE = (384, 768)
KEEP = tuple(PART - share for share in SHARE)
FF = 384
LENGTH = EXPERTS * ROWS
RIGHT, OPPOSITE, LEFT = 1, 2, 3
SEMAPHORES = 138
ORDER = (0, 4, 1, 5, 2, 6, 3, 7)


def rope_table(length):
    freqs = THETA ** (-2.0 * np.arange(HS // 2) / HS)
    angles = np.arange(length)[:, None] * freqs[None, :]
    cosine, sine = np.cos(angles), np.sin(angles)
    return np.concatenate([cosine, cosine, -sine, sine], axis=1).astype(np.float32)


class Group:
    def __init__(self, sem, whole):
        self.sem, self.whole, self.sent, self.waited = sem, whole, False, False


class Messages:
    def __init__(self, sems):
        self.sems, self.used, self.sends, self.recvs = sems, 0, [], []

    def group(self, whole, kind):
        found = Group(self.sems.at[self.used], whole)
        self.used += 1
        kind.append(found)
        return found

    def leaving(self, whole):
        return self.group(whole, self.sends)

    def coming(self, whole):
        return self.group(whole, self.recvs)

    def send(self, src, dst, leaving, coming, **where):
        pltpu.make_async_remote_copy(
            src_ref=src,
            dst_ref=dst,
            send_sem=leaving.sem,
            recv_sem=coming.sem,
            device_id=where,
            device_id_type=MESH,
        ).start()
        leaving.sent = coming.sent = True

    def _any(self, found):
        return pltpu.make_async_remote_copy(
            src_ref=found.whole,
            dst_ref=found.whole,
            send_sem=found.sem,
            recv_sem=found.sem,
            device_id={"tensor": lax.rem(lax.axis_index("tensor") + 1, 4)},
            device_id_type=MESH,
        )

    def wait(self, found):
        self._any(found).wait_recv()
        found.waited = True

    def finish(self):
        for found in self.recvs:
            if found.sent and not found.waited:
                self.wait(found)
        for found in self.sends:
            if found.sent:
                self._any(found).wait_send()


def dot(a, b):
    return jnp.dot(a, b, preferred_element_type=F32)


def dot_first(a, b):
    return lax.dot_general(a, b, (((0,), (0,)), ((), ())), preferred_element_type=F32)


def flipped(line):
    n = max(line.shape)
    diagonal = lax.broadcasted_iota(jnp.int32, (n, n), 0) == lax.broadcasted_iota(
        jnp.int32, (n, n), 1
    )
    axis = 0 if line.shape[1] == 1 else 1
    return jnp.sum(jnp.where(diagonal, line, 0.0), axis=axis, keepdims=True)


def encoded(value):
    highest = jnp.maximum(jnp.max(jnp.abs(value), axis=1, keepdims=True), 1e-30)
    codes = jnp.round(value * (32760.0 / highest)).astype(jnp.int32).astype(I16)
    return codes, highest * (1.0 / 32760.0)


def decoded(codes, step):
    return codes.astype(jnp.int32).astype(F32) * step


def kernel(
    stream_hbm, ids_hbm, gates_hbm, mgain_hbm, again_hbm,
    wg_hbm, wu_hbm, wd_hbm, wq_hbm, wkv_hbm, rope_hbm,
    moe_out, context_out,
    stream, ids, gates, mgain, again, w13, wd, wqkv, wkv, rope,
    ssq, gains, raw0, raw1, out0, out1, x0, x1, out_all0, out_all1, x_all0, x_all1, rates_out, rates_in, acc, hidden,
    opp, going_r, going_l, part_r, part_l, own, opp_l, opp_r, sum_l, sum_r,
    steps_r, steps_l, steps_from_r, steps_from_l, more_r, more_l, more_from_r, more_from_l,
    eo, ret, mixed, rows_in, kv_own, kv_in, context,
    local_sems, sems,
):
    e, t, p = lax.axis_index("expert"), lax.axis_index("tensor"), lax.axis_index("pipe")
    right, left, opposite = lax.rem(t + 1, 4), lax.rem(t + 3, 4), lax.rem(t + 2, 4)
    after, before = lax.rem(p + 1, 8), lax.rem(p + 7, 8)
    peer = [lax.rem(e + o, EXPERTS) for o in range(EXPERTS)]
    msg = Messages(sems)
    raw, out, x = (raw0, raw1), (out0, out1), (x0, x1)
    out_all, x_all = (out_all0, out_all1), (x_all0, x_all1)

    here = pl.ds(pl.multiple_of(e * ROWS, ROWS), ROWS)
    loads = [
        (stream_hbm, stream),
        (ids_hbm, ids),
        (mgain_hbm, mgain),
        (gates_hbm, gates),
        (again_hbm, again),
        (wg_hbm, w13.at[:, :FF]),
        (wu_hbm, w13.at[:, FF:]),
        (wd_hbm, wd),
        (wq_hbm, wqkv.at[:, :HS]),
        (wkv_hbm, wkv),
        (rope_hbm.at[here], rope),
    ]
    loads = [pltpu.make_async_copy(s, d, local_sems.at[i]) for i, (s, d) in enumerate(loads)]
    for load in loads:
        load.start()

    barrier = pltpu.get_barrier_semaphore()
    peers = [{"expert": other} for other in peer[1:]]
    peers += [{"tensor": other} for other in (right, left, opposite)]
    peers += [{"pipe": other} for other in (after, before)]
    for other in peers:
        pl.semaphore_signal(barrier, inc=1, device_id=other, device_id_type=MESH)

    slot = lax.broadcasted_iota(jnp.int32, (SLOTS, ROWS), 0)
    group, place = slot // CAP, slot % CAP
    expert_of = jnp.where(group + e >= EXPERTS, group + e - EXPERTS, group + e)
    row_of = lax.broadcasted_iota(jnp.int32, (ROWS, ROWS), 0)
    col_of = lax.broadcasted_iota(jnp.int32, (ROWS, ROWS), 1)
    earlier = jnp.where(row_of < col_of, 1.0, 0.0).astype(BF16)
    for load in loads[:5]:
        load.wait()
    chosen = []
    for m in range(MICRO):
        first = ids[m, 0:1, :] == expert_of
        second = ids[m, 1:2, :] == expert_of
        named = jnp.where(first | second, 1.0, 0.0)
        taken = dot(named.astype(BF16), earlier) == place.astype(F32)
        chosen.append(
            [jnp.where(which & taken, 1.0, 0.0).astype(BF16) for which in (first, second)]
        )

    value = stream[...].reshape(MICRO * ROWS, PART).astype(F32)
    ssq[0] = jnp.broadcast_to(flipped(jnp.sum(value * value, axis=1, keepdims=True)), (8, MICRO * ROWS))
    gains[0, :8] = jnp.broadcast_to(mgain[...], (8, PART))
    gains[0, 8:] = jnp.broadcast_to(again[...], (8, PART))
    for m in range(MICRO):
        raw[m][0] = stream[m, :, KEEP[m] :]

    pl.semaphore_wait(barrier, len(peers))

    def to_tensor_peers(buffer):
        leaving, coming = msg.leaving(buffer.at[1:4]), msg.coming(buffer.at[1:4])
        for rel, other in ((RIGHT, right), (LEFT, left), (OPPOSITE, opposite)):
            msg.send(buffer.at[0], buffer.at[rel], leaving, coming, tensor=other)
        return coming

    out_leave = [msg.leaving(out[m].at[1:]) for m in range(MICRO)]
    out_come = [[None] + [msg.coming(x[m].at[0, o]) for o in range(1, EXPERTS)] for m in range(MICRO)]
    all_leave = [msg.leaving(out_all[m].at[1:]) for m in range(MICRO)]
    all_come = [msg.coming(x_all[m].at[1:]) for m in range(MICRO)]
    rates_leave, rates_come = msg.leaving(rates_out.at[1:]), msg.coming(rates_in.at[1:])
    x_leave_r = [msg.leaving(x[m].at[0]) for m in range(MICRO)]
    x_leave_l = [msg.leaving(x[m].at[0]) for m in range(MICRO)]
    near = EXPERTS // 2
    x_come_r = [
        [msg.coming(x[m].at[RIGHT, o]) for o in range(near)] + [msg.coming(x[m].at[RIGHT, near:])] * near
        for m in range(MICRO)
    ]
    x_come_l = [
        [msg.coming(x[m].at[LEFT, :near])] * near + [msg.coming(x[m].at[LEFT, o]) for o in range(near, EXPERTS)]
        for m in range(MICRO)
    ]
    ahead_leave_r = [msg.leaving(x[m].at[RIGHT, :near]) for m in range(MICRO)]
    ahead_leave_l = [msg.leaving(x[m].at[LEFT, near:]) for m in range(MICRO)]
    ahead_come_r = [msg.coming(x[m].at[OPPOSITE, :near]) for m in range(MICRO)]
    ahead_come_l = [msg.coming(x[m].at[OPPOSITE, near:]) for m in range(MICRO)]

    placing = [chosen[m][0] + chosen[m][1] for m in range(MICRO)]

    def dispatch(m):
        block = dot(placing[m], stream[m, :, : KEEP[m]]).astype(BF16).reshape(EXPERTS, CAP, KEEP[m])
        x[m][0, 0] = block[0]
        out[m][...] = block
        for o in ORDER[1:]:
            msg.send(out[m].at[o], x[m].at[0, o], out_leave[m], out_come[m][o], expert=peer[o])

    def dispatch_all(m):
        for rel in range(4):
            at = slice(rel * SHARE[m], (rel + 1) * SHARE[m])
            block = dot(placing[m], raw[m][rel]).astype(BF16).reshape(EXPERTS, CAP, SHARE[m])
            x_all[m][0, :, at] = block[0]
            out_all[m][:, :, at] = block
        for o in range(1, EXPERTS):
            msg.send(out_all[m].at[o], x_all[m].at[o], all_leave[m], all_come[m], expert=peer[o])

    def dispatch_rates():
        total = (ssq[0, 0:1, :] + ssq[1, 0:1, :]) + (ssq[2, 0:1, :] + ssq[3, 0:1, :])
        scales = lax.rsqrt(total * (1.0 / (4 * PART)) + EPS)
        rates_out[...] = jnp.zeros(rates_out.shape, F32)
        for m in range(MICRO):
            scale = scales[:, m * ROWS : (m + 1) * ROWS]
            rate = jnp.sum(placing[m].astype(F32) * scale, axis=1, keepdims=True)
            for o in range(EXPERTS):
                rates_out[o, m : m + 1, :CAP] = flipped(rate[o * CAP : (o + 1) * CAP])
        rates_in[0] = rates_out[0]
        for o in range(1, EXPERTS):
            msg.send(rates_out.at[o], rates_in.at[o], rates_leave, rates_come, expert=peer[o])

    def rates_of(m):
        return jnp.concatenate(
            [flipped(rates_in[o, m : m + 1, :CAP]) for o in range(EXPERTS)], axis=0
        )

    def gather_send(m, pieces):
        for o in pieces:
            if o > 0:
                msg.wait(out_come[m][o])
            msg.send(x[m].at[0, o], x[m].at[RIGHT, o], x_leave_r[m], x_come_r[m][o], tensor=right)
            msg.send(x[m].at[0, o], x[m].at[LEFT, o], x_leave_l[m], x_come_l[m][o], tensor=left)

    def gather_forward(m):
        for i in range(near):
            msg.wait(x_come_r[m][i])
            msg.send(x[m].at[RIGHT, i], x[m].at[OPPOSITE, i], ahead_leave_r[m], ahead_come_r[m], tensor=right)
            o = i + near
            msg.wait(x_come_l[m][o])
            msg.send(x[m].at[LEFT, o], x[m].at[OPPOSITE, o], ahead_leave_l[m], ahead_come_l[m], tensor=left)

    def columns_of(rel, first, width):
        return pl.ds(pl.multiple_of(lax.rem(t + 4 - rel, 4) * PART + first, HS), width)

    def normed_rows(rows, rate, gain):
        return (rows.astype(F32) * rate * gain.astype(F32)).astype(BF16)

    def expert_in(m, rel):
        rows = x[m][rel].reshape(SLOTS, KEEP[m])
        normed = normed_rows(rows, rates_of(m), gains[rel, 0:1, : KEEP[m]])
        value = dot(normed, w13[columns_of(rel, 0, KEEP[m]), :])
        acc[...] = value if rel == 0 else acc[...] + value

    def expert_in_all(m):
        value = None
        for rel in range(4):
            rows = x_all[m][:, :, rel * SHARE[m] : (rel + 1) * SHARE[m]].reshape(SLOTS, SHARE[m])
            normed = normed_rows(rows, rates_of(m), gains[rel, 0:1, KEEP[m] :])
            term = dot(normed, w13[columns_of(rel, KEEP[m], SHARE[m]), :])
            value = term if value is None else value + term
        acc[...] += value

    def activate(m):
        gated, lifted = acc[:, :FF], acc[:, FF:]
        hidden[m] = (gated / (1.0 + jnp.exp(-gated)) * lifted).astype(BF16)

    def pairs(buffer, kind):
        return [kind(buffer.at[m]) for m in range(MICRO)]

    def each(buffer, rows):
        return [[msg.coming(buffer.at[m, c, rows]) for c in range(CUTS)] for m in range(MICRO)]

    top, low, every = slice(0, HALF), slice(HALF, SLOTS), slice(None)
    opp_leave, going_r_leave, going_l_leave = (
        pairs(b, msg.leaving) for b in (opp, going_r, going_l)
    )
    steps_r_leave, steps_l_leave, more_r_leave, more_l_leave = (
        pairs(b, msg.leaving) for b in (steps_r, steps_l, more_r, more_l)
    )
    opp_l_come, opp_r_come = each(opp_l, every), each(opp_r, every)
    sum_l_top, sum_l_low = each(sum_l, top), each(sum_l, low)
    sum_r_top, sum_r_low = each(sum_r, top), each(sum_r, low)
    steps_l_come, steps_r_come = each(steps_from_l, every), each(steps_from_r, every)
    more_l_come, more_r_come = each(more_from_l, every), each(more_from_r, every)

    def part(m, c, rel):
        at = pl.multiple_of(lax.rem(t + rel, 4) * PART + c * WIDE, WIDE)
        return dot(hidden[m], wd[:, pl.ds(at, WIDE)])

    def send_opposite(m, c):
        opp[m, c], step = encoded(part(m, c, OPPOSITE))
        for ref in (steps_r, steps_l, more_r, more_l):
            ref[m, c] = jnp.zeros((8, HALF), F32)
        steps_r[m, c, 0:1] = flipped(step[:HALF])
        steps_l[m, c, 0:1] = flipped(step[HALF:])
        msg.send(opp.at[m, c, top], opp_l.at[m, c], opp_leave[m], opp_l_come[m][c], tensor=right)
        msg.send(opp.at[m, c, low], opp_r.at[m, c], opp_leave[m], opp_r_come[m][c], tensor=left)

    def send_direct(m, c):
        value = part(m, c, RIGHT)
        part_r[m, c] = value[:HALF]
        going_r[m, c, low], step = encoded(value[HALF:])
        steps_r[m, c, 1:2] = flipped(step)
        msg.send(steps_r.at[m, c], steps_from_l.at[m, c], steps_r_leave[m], steps_l_come[m][c], tensor=right)
        msg.send(going_r.at[m, c, low], sum_l.at[m, c, low], going_r_leave[m], sum_l_low[m][c], tensor=right)
        value = part(m, c, LEFT)
        part_l[m, c] = value[HALF:]
        going_l[m, c, top], step = encoded(value[:HALF])
        steps_l[m, c, 1:2] = flipped(step)
        msg.send(steps_l.at[m, c], steps_from_r.at[m, c], steps_l_leave[m], steps_r_come[m][c], tensor=left)
        msg.send(going_l.at[m, c, top], sum_r.at[m, c, top], going_l_leave[m], sum_r_top[m][c], tensor=left)

    def sum_middle(m, c):
        msg.wait(steps_l_come[m][c])
        msg.wait(opp_l_come[m][c])
        value = part_r[m, c] + decoded(opp_l[m, c], flipped(steps_from_l[m, c, 0:1]))
        going_r[m, c, top], step = encoded(value)
        more_r[m, c, 0:1] = flipped(step)
        msg.send(more_r.at[m, c], more_from_l.at[m, c], more_r_leave[m], more_l_come[m][c], tensor=right)
        msg.send(going_r.at[m, c, top], sum_l.at[m, c, top], going_r_leave[m], sum_l_top[m][c], tensor=right)
        msg.wait(steps_r_come[m][c])
        msg.wait(opp_r_come[m][c])
        value = part_l[m, c] + decoded(opp_r[m, c], flipped(steps_from_r[m, c, 0:1]))
        going_l[m, c, low], step = encoded(value)
        more_l[m, c, 0:1] = flipped(step)
        msg.send(more_l.at[m, c], more_from_r.at[m, c], more_l_leave[m], more_r_come[m][c], tensor=left)
        msg.send(going_l.at[m, c, low], sum_r.at[m, c, low], going_l_leave[m], sum_r_low[m][c], tensor=left)

    eo_leave = [msg.leaving(eo.at[m, :, 1:]) for m in range(MICRO)]
    ret_come = [[msg.coming(ret.at[m, c, 1:]) for c in range(CUTS)] for m in range(MICRO)]

    def sum_last(m, c):
        for found in (sum_l_low, sum_r_top, more_l_come, sum_l_top, more_r_come, sum_r_low):
            msg.wait(found[m][c])
        above = own[m, c, top] + (
            decoded(sum_l[m, c, top], flipped(more_from_l[m, c, 0:1]))
            + decoded(sum_r[m, c, top], flipped(steps_from_r[m, c, 1:2]))
        )
        below = own[m, c, low] + (
            decoded(sum_l[m, c, low], flipped(steps_from_l[m, c, 1:2]))
            + decoded(sum_r[m, c, low], flipped(more_from_r[m, c, 0:1]))
        )
        value = jnp.concatenate([above.astype(BF16), below.astype(BF16)], axis=0)
        value = value.reshape(EXPERTS, CAP, WIDE)
        ret[m, c, 0] = value[0]
        eo[m, c] = value
        for o in range(1, EXPERTS):
            msg.send(
                eo.at[m, c, o], ret.at[m, c, o], eo_leave[m], ret_come[m][c],
                expert=lax.rem(e + EXPERTS - o, EXPERTS),
            )

    mixed_leave = [msg.leaving(mixed.at[m]) for m in range(MICRO)]
    moe_writes = []
    shift_come = [[msg.coming(rows_in.at[m, 0, c]) for c in range(CUTS)] for m in range(MICRO)]

    def combine(m, c):
        msg.wait(ret_come[m][c])
        returned = ret[m, c].reshape(SLOTS, WIDE)
        columns = slice(c * WIDE, (c + 1) * WIDE)
        value = None
        for k in range(2):
            term = flipped(gates[m, k : k + 1, :]) * dot_first(chosen[m][k], returned)
            value = term if value is None else value + term
        mixed[m, c] = (stream[m, :, columns].astype(F32) + value).astype(BF16)
        msg.send(mixed.at[m, c], rows_in.at[m, 0, c], mixed_leave[m], shift_come[m][c], pipe=after)
        number = len(loads) + len(moe_writes)
        moe_writes.append(
            pltpu.make_async_copy(mixed.at[m, c], moe_out.at[m, :, columns], local_sems.at[number])
        )
        moe_writes[-1].start()

    rows_leave = [msg.leaving(rows_in.at[m, 1:]) for m in range(MICRO)]
    rows_come = [[msg.coming(rows_in.at[m, 1:, c]) for c in range(CUTS)] for m in range(MICRO)]

    def rows_send(m, c):
        msg.wait(shift_come[m][c])
        for rel, other in ((OPPOSITE, opposite), (RIGHT, right), (LEFT, left)):
            msg.send(
                rows_in.at[m, 0, c], rows_in.at[m, rel, c], rows_leave[m], rows_come[m][c], tensor=other
            )

    kv_leave = [msg.leaving(kv_in.at[m, 1:]) for m in range(MICRO)]
    kv_come = [msg.coming(kv_in.at[m, 1:]) for m in range(MICRO)]

    def turned(value):
        swapped = pltpu.roll(value, HS // 2, 1)
        return (value * rope[:, :HS] + swapped * rope[:, HS:]).astype(BF16)

    def project(m):
        for c in range(CUTS):
            msg.wait(rows_come[m][c])
        total = None
        for rel in range(4):
            for c in range(CUTS):
                value = rows_in[m, rel, c].astype(F32)
                term = jnp.sum(value * value, axis=-1, keepdims=True)
                total = term if total is None else total + term
        scale = lax.rsqrt(total * (1.0 / (4 * PART)) + EPS)
        result = None
        for rel in range(4):
            for c in range(CUTS):
                gain = gains[rel, 8:9, c * WIDE : (c + 1) * WIDE].astype(F32)
                normed = (rows_in[m, rel, c].astype(F32) * scale * gain).astype(BF16)
                at = pl.multiple_of(lax.rem(t + 4 - rel, 4) * PART + c * WIDE, WIDE)
                term = dot(normed, wqkv[pl.ds(at, WIDE), :])
                result = term if result is None else result + term
        query = turned(result[:, :HS])
        key = turned(result[:, HS : 2 * HS])
        kv = jnp.concatenate([key, result[:, 2 * HS :].astype(BF16)], axis=1)
        kv_own[m] = kv
        kv_in[m, 0] = kv
        for o in range(1, EXPERTS):
            msg.send(kv_own.at[m], kv_in.at[m, o], kv_leave[m], kv_come[m], expert=peer[o])
        return query

    def attend(m, query):
        column = lax.broadcasted_iota(jnp.int32, (ROWS, LENGTH), 1)
        source = e - column // ROWS
        source = jnp.where(source < 0, source + EXPERTS, source)
        row = e * ROWS + lax.broadcasted_iota(jnp.int32, (ROWS, LENGTH), 0)
        causal = source * ROWS + column % ROWS <= row
        msg.wait(kv_come[m])
        kv = kv_in[m].reshape(LENGTH, 2 * HS)
        scores = lax.dot_general(
            query, kv[:, :HS], (((1,), (1,)), ((), ())), preferred_element_type=F32
        )
        scores = jnp.where(causal, scores * HS ** (-0.5), NEGATIVE)
        highest = jnp.max(scores, axis=-1, keepdims=True)
        weights = jnp.where(causal, jnp.exp(scores - highest), 0.0)
        total = jnp.sum(weights, axis=-1, keepdims=True)
        context[m] = (dot(weights.astype(BF16), kv[:, HS:]) / total).astype(BF16)

    def split_weights():
        step = 512
        row = lax.broadcasted_iota(jnp.int32, (step // 2, step), 0)
        col = lax.broadcasted_iota(jnp.int32, (step // 2, step), 1)

        def body(i, _):
            block = wkv[pl.ds(pl.multiple_of(i * step, step), step), :]
            to = pl.ds(pl.multiple_of(i * (step // 2), step // 2), step // 2)
            for k in range(2):
                pick = jnp.where(col == 2 * row + k, 1.0, 0.0).astype(BF16)
                wqkv[to, (k + 1) * HS : (k + 2) * HS] = dot(pick, block).astype(BF16)
            return 0

        lax.fori_loop(0, wkv.shape[0] // step, body, 0)

    raw_come = [to_tensor_peers(raw[0])]
    dispatch(0)
    gather_send(0, [0])
    dispatch(1)
    ssq_come = to_tensor_peers(ssq)
    raw_come.append(to_tensor_peers(raw[1]))
    gains_come = to_tensor_peers(gains)
    msg.wait(raw_come[0])
    dispatch_all(0)
    gather_send(0, ORDER[1:5])
    msg.wait(ssq_come)
    dispatch_rates()
    gather_send(0, ORDER[5:])
    gather_forward(0)
    msg.wait(raw_come[1])
    dispatch_all(1)
    gather_send(1, ORDER)
    for load in loads[5:]:
        load.wait()
    msg.wait(rates_come)
    msg.wait(gains_come)
    expert_in(0, 0)
    msg.wait(x_come_r[0][near])
    expert_in(0, RIGHT)
    msg.wait(x_come_l[0][0])
    expert_in(0, LEFT)
    msg.wait(ahead_come_r[0])
    msg.wait(ahead_come_l[0])
    expert_in(0, OPPOSITE)
    msg.wait(all_come[0])
    expert_in_all(0)
    activate(0)
    for c in range(CUTS):
        send_opposite(0, c)
        send_direct(0, c)
    gather_forward(1)
    for c in range(CUTS):
        own[0, c] = part(0, c, 0)
        sum_middle(0, c)
    expert_in(1, 0)
    split_weights()
    msg.wait(x_come_r[1][near])
    expert_in(1, RIGHT)
    msg.wait(x_come_l[1][0])
    expert_in(1, LEFT)
    msg.wait(ahead_come_r[1])
    msg.wait(ahead_come_l[1])
    expert_in(1, OPPOSITE)
    msg.wait(all_come[1])
    expert_in_all(1)
    activate(1)
    send_opposite(1, 0)
    send_direct(1, 0)
    send_opposite(1, 1)
    sum_last(0, 0)
    sum_middle(1, 0)
    send_direct(1, 1)
    sum_last(0, 1)
    for c in range(CUTS):
        own[1, c] = part(1, c, 0)
    sum_middle(1, 1)
    combine(0, 0)
    combine(0, 1)
    sum_last(1, 0)
    rows_send(0, 0)
    rows_send(0, 1)
    sum_last(1, 1)
    combine(1, 0)
    query0 = project(0)
    combine(1, 1)
    rows_send(1, 0)
    rows_send(1, 1)
    attend(0, query0)
    query1 = project(1)
    attend(1, query1)

    writes = [
        pltpu.make_async_copy(context, context_out, local_sems.at[len(loads) + len(moe_writes)])
    ]
    writes[0].start()
    for write in writes + moe_writes:
        write.wait()
    msg.finish()


def per_device(
    stream, expert_ids, expert_gates, moe_gain, w_gate, w_up, w_down, attn_gain, w_query, w_keyval
):
    hbm = pl.BlockSpec(memory_space=pl.ANY)
    slots_cut = (MICRO, CUTS, SLOTS, WIDE)
    half_cut = (MICRO, CUTS, HALF, WIDE)
    scratch = [
        ((MICRO, ROWS, PART), BF16),
        ((MICRO, 2, ROWS), jnp.int32),
        ((MICRO, 2, ROWS), F32),
        ((1, PART), BF16),
        ((1, PART), BF16),
        ((4 * PART, 2 * FF), BF16),
        ((FF, 4 * PART), BF16),
        ((4 * PART, 3 * HS), BF16),
        ((8 * PART, HS), BF16),
        ((ROWS, 2 * HS), F32),
        ((4, 8, MICRO * ROWS), F32),
        ((4, 16, PART), BF16),
        *(((4, ROWS, SHARE[m]), BF16) for m in range(MICRO)),
        *(((EXPERTS, CAP, KEEP[m]), BF16) for m in range(MICRO)),
        *(((4, EXPERTS, CAP, KEEP[m]), BF16) for m in range(MICRO)),
        *(((EXPERTS, CAP, 4 * SHARE[m]), BF16) for m in (0, 1, 0, 1)),
        ((EXPERTS, 8, HS), F32),
        ((EXPERTS, 8, HS), F32),
        ((SLOTS, 2 * FF), F32),
        ((MICRO, SLOTS, FF), BF16),
        (slots_cut, I16),
        (slots_cut, I16),
        (slots_cut, I16),
        (half_cut, F32),
        (half_cut, F32),
        (slots_cut, F32),
        (half_cut, I16),
        (half_cut, I16),
        (slots_cut, I16),
        (slots_cut, I16),
    ]
    scratch += [((MICRO, CUTS, 8, HALF), F32)] * 8
    scratch += [
        ((MICRO, CUTS, EXPERTS, CAP, WIDE), BF16),
        ((MICRO, CUTS, EXPERTS, CAP, WIDE), BF16),
        ((MICRO, CUTS, ROWS, WIDE), BF16),
        ((MICRO, 4, CUTS, ROWS, WIDE), BF16),
        ((MICRO, ROWS, 2 * HS), BF16),
        ((MICRO, EXPERTS, ROWS, 2 * HS), BF16),
        ((MICRO, ROWS, HS), BF16),
    ]
    moe, context = pl.pallas_call(
        kernel,
        out_shape=(
            jax.ShapeDtypeStruct((MICRO, ROWS, PART), BF16),
            jax.ShapeDtypeStruct((MICRO, ROWS, HS), BF16),
        ),
        in_specs=[hbm] * 11,
        out_specs=(hbm, hbm),
        scratch_shapes=[pltpu.VMEM(shape, kind) for shape, kind in scratch]
        + [pltpu.SemaphoreType.DMA((16,)), pltpu.SemaphoreType.DMA((SEMAPHORES,))],
        compiler_params=pltpu.CompilerParams(
            collective_id=0, has_side_effects=True, vmem_limit_bytes=56 * 1024 * 1024
        ),
        cost_estimate=pl.CostEstimate(
            flops=5_300_000_000, bytes_accessed=13_000_000, transcendentals=500_000
        ),
    )(
        stream[0],
        jnp.transpose(expert_ids[0], (0, 2, 1)),
        jnp.transpose(expert_gates[0], (0, 2, 1)),
        moe_gain,
        attn_gain,
        w_gate[0, 0],
        w_up[0, 0],
        w_down[0, 0],
        w_query[0],
        w_keyval[0].reshape(8 * PART, HS),
        jnp.asarray(rope_table(LENGTH)),
    )
    return moe[None], context[None]


def solution(mesh):
    placed = (
        P("pipe", None, "expert", "tensor"),
        P("pipe", None, "expert", None),
        P("pipe", None, "expert", None),
        P("pipe", "tensor"),
        P("pipe", "expert", None, "tensor"),
        P("pipe", "expert", None, "tensor"),
        P("pipe", "expert", "tensor", None),
        P("pipe", "tensor"),
        P("pipe", None, "tensor"),
        P("pipe", None, None, "tensor"),
    )
    return jax.shard_map(
        per_device,
        mesh=mesh,
        in_specs=placed,
        out_specs=(P("pipe", None, "expert", "tensor"), P("pipe", None, "expert", "tensor")),
        check_vma=False,
    )
```

```python
import jax
import jax.numpy as jnp
import numpy as np
from jax import lax
from jax.experimental import pallas as pl
from jax.experimental.pallas import tpu as pltpu
from jax.sharding import PartitionSpec as P

MESH = pl.DeviceIdType.MESH
HS = 128
EPS = 1e-05
THETA = 1000000.0
NEGATIVE = -1e30
F32 = jnp.float32
BF16 = jnp.bfloat16
I16 = jnp.int16

MICRO = 2
ROWS = 64
PART = 1024
CAP = 32
EXPERTS = 8
SLOTS = EXPERTS * CAP
HALF = SLOTS // 2
CUTS = 2
WIDE = PART // CUTS
SHARE = (384, 768)
KEEP = tuple(PART - share for share in SHARE)
FF = 384
LENGTH = EXPERTS * ROWS
RIGHT, OPPOSITE, LEFT = 1, 2, 3
SEMAPHORES = 144
ORDER = (0, 4, 1, 5, 2, 6, 3, 7)


def rope_table(length):
    freqs = THETA ** (-2.0 * np.arange(HS // 2) / HS)
    angles = np.arange(length)[:, None] * freqs[None, :]
    cosine, sine = np.cos(angles), np.sin(angles)
    return np.concatenate([cosine, cosine, -sine, sine], axis=1).astype(np.float32)


class Group:
    def __init__(self, sem, whole):
        self.sem, self.whole, self.sent, self.waited = sem, whole, False, False


class Messages:
    def __init__(self, sems):
        self.sems, self.used, self.sends, self.recvs = sems, 0, [], []

    def group(self, whole, kind):
        found = Group(self.sems.at[self.used], whole)
        self.used += 1
        kind.append(found)
        return found

    def leaving(self, whole):
        return self.group(whole, self.sends)

    def coming(self, whole):
        return self.group(whole, self.recvs)

    def send(self, src, dst, leaving, coming, **where):
        pltpu.make_async_remote_copy(
            src_ref=src,
            dst_ref=dst,
            send_sem=leaving.sem,
            recv_sem=coming.sem,
            device_id=where,
            device_id_type=MESH,
        ).start()
        leaving.sent = coming.sent = True

    def _any(self, found):
        return pltpu.make_async_remote_copy(
            src_ref=found.whole,
            dst_ref=found.whole,
            send_sem=found.sem,
            recv_sem=found.sem,
            device_id={"tensor": lax.rem(lax.axis_index("tensor") + 1, 4)},
            device_id_type=MESH,
        )

    def wait(self, found):
        self._any(found).wait_recv()
        found.waited = True

    def finish(self):
        for found in self.recvs:
            if found.sent and not found.waited:
                self.wait(found)
        for found in self.sends:
            if found.sent:
                self._any(found).wait_send()


def dot(a, b):
    return jnp.dot(a, b, preferred_element_type=F32)


def dot_first(a, b):
    return lax.dot_general(a, b, (((0,), (0,)), ((), ())), preferred_element_type=F32)


def flipped(line):
    n = max(line.shape)
    diagonal = lax.broadcasted_iota(jnp.int32, (n, n), 0) == lax.broadcasted_iota(
        jnp.int32, (n, n), 1
    )
    axis = 0 if line.shape[1] == 1 else 1
    return jnp.sum(jnp.where(diagonal, line, 0.0), axis=axis, keepdims=True)


def encoded(value):
    highest = jnp.maximum(jnp.max(jnp.abs(value), axis=1, keepdims=True), 1e-30)
    codes = jnp.round(value * (32760.0 / highest)).astype(jnp.int32).astype(I16)
    return codes, highest * (1.0 / 32760.0)


def decoded(codes, step):
    return codes.astype(jnp.int32).astype(F32) * step


def kernel(
    stream_hbm, ids_hbm, gates_hbm, mgain_hbm, again_hbm,
    wg_hbm, wu_hbm, wd_hbm, wq_hbm, wkv_hbm, rope_hbm,
    moe_out, context_out,
    stream, ids, gates, mgain, again, w13, wd, wqkv, wkv, rope,
    ssq, gains, raw0, raw1, out0, out1, x0, x1, out_all0, out_all1, x_all0, x_all1, rates_out, rates_in, acc, hidden,
    opp, going_r, going_l, part_r, part_l, own, opp_l, opp_r, sum_l, sum_r,
    steps_r, steps_l, steps_from_r, steps_from_l, more_r, more_l, more_from_r, more_from_l,
    eo, ret, mixed, rows_in, kv_own, kv_in, context,
    local_sems, sems,
):
    e, t, p = lax.axis_index("expert"), lax.axis_index("tensor"), lax.axis_index("pipe")
    right, left, opposite = lax.rem(t + 1, 4), lax.rem(t + 3, 4), lax.rem(t + 2, 4)
    after, before = lax.rem(p + 1, 8), lax.rem(p + 7, 8)
    peer = [lax.rem(e + o, EXPERTS) for o in range(EXPERTS)]
    msg = Messages(sems)
    raw, out, x = (raw0, raw1), (out0, out1), (x0, x1)
    out_all, x_all = (out_all0, out_all1), (x_all0, x_all1)

    here = pl.ds(pl.multiple_of(e * ROWS, ROWS), ROWS)
    loads = [
        (stream_hbm, stream),
        (ids_hbm, ids),
        (mgain_hbm, mgain),
        (gates_hbm, gates),
        (again_hbm, again),
        (wg_hbm, w13.at[:, :FF]),
        (wu_hbm, w13.at[:, FF:]),
        (wd_hbm, wd),
        (wq_hbm, wqkv.at[:, :HS]),
        (wkv_hbm, wkv),
        (rope_hbm.at[here], rope),
    ]
    loads = [pltpu.make_async_copy(s, d, local_sems.at[i]) for i, (s, d) in enumerate(loads)]
    for load in loads:
        load.start()

    barrier = pltpu.get_barrier_semaphore()
    peers = [{"expert": other} for other in peer[1:]]
    peers += [{"tensor": other} for other in (right, left, opposite)]
    peers += [{"pipe": other} for other in (after, before)]
    for other in peers:
        pl.semaphore_signal(barrier, inc=1, device_id=other, device_id_type=MESH)

    slot = lax.broadcasted_iota(jnp.int32, (SLOTS, ROWS), 0)
    group, place = slot // CAP, slot % CAP
    expert_of = jnp.where(group + e >= EXPERTS, group + e - EXPERTS, group + e)
    row_of = lax.broadcasted_iota(jnp.int32, (ROWS, ROWS), 0)
    col_of = lax.broadcasted_iota(jnp.int32, (ROWS, ROWS), 1)
    earlier = jnp.where(row_of < col_of, 1.0, 0.0).astype(BF16)
    for load in loads[:5]:
        load.wait()
    chosen = []
    for m in range(MICRO):
        first = ids[m, 0:1, :] == expert_of
        second = ids[m, 1:2, :] == expert_of
        named = jnp.where(first | second, 1.0, 0.0)
        taken = dot(named.astype(BF16), earlier) == place.astype(F32)
        chosen.append(
            [jnp.where(which & taken, 1.0, 0.0).astype(BF16) for which in (first, second)]
        )

    value = stream[...].reshape(MICRO * ROWS, PART).astype(F32)
    ssq[0] = jnp.broadcast_to(flipped(jnp.sum(value * value, axis=1, keepdims=True)), (8, MICRO * ROWS))
    gains[0, :8] = jnp.broadcast_to(mgain[...], (8, PART))
    gains[0, 8:] = jnp.broadcast_to(again[...], (8, PART))
    for m in range(MICRO):
        raw[m][0] = stream[m, :, KEEP[m] :]

    pl.semaphore_wait(barrier, len(peers))

    def to_tensor_peers(buffer):
        leaving, coming = msg.leaving(buffer.at[1:4]), msg.coming(buffer.at[1:4])
        for rel, other in ((RIGHT, right), (LEFT, left), (OPPOSITE, opposite)):
            msg.send(buffer.at[0], buffer.at[rel], leaving, coming, tensor=other)
        return coming

    out_leave = [msg.leaving(out[m].at[1:]) for m in range(MICRO)]
    out_come = [[None] + [msg.coming(x[m].at[0, o]) for o in range(1, EXPERTS)] for m in range(MICRO)]
    all_leave = [msg.leaving(out_all[m].at[1:]) for m in range(MICRO)]
    shares = [[slice(r * SHARE[m], (r + 1) * SHARE[m]) for r in range(4)] for m in range(MICRO)]
    all_come = [[msg.coming(x_all[m].at[1:, :, at]) for at in shares[m]] for m in range(MICRO)]
    rates_leave, rates_come = msg.leaving(rates_out.at[1:]), msg.coming(rates_in.at[1:])
    x_leave_r = [msg.leaving(x[m].at[0]) for m in range(MICRO)]
    x_leave_l = [msg.leaving(x[m].at[0]) for m in range(MICRO)]
    near = EXPERTS // 2
    x_come_r = [
        [msg.coming(x[m].at[RIGHT, o]) for o in range(near)] + [msg.coming(x[m].at[RIGHT, near:])] * near
        for m in range(MICRO)
    ]
    x_come_l = [
        [msg.coming(x[m].at[LEFT, :near])] * near + [msg.coming(x[m].at[LEFT, o]) for o in range(near, EXPERTS)]
        for m in range(MICRO)
    ]
    ahead_leave_r = [msg.leaving(x[m].at[RIGHT, :near]) for m in range(MICRO)]
    ahead_leave_l = [msg.leaving(x[m].at[LEFT, near:]) for m in range(MICRO)]
    ahead_come_r = [msg.coming(x[m].at[OPPOSITE, :near]) for m in range(MICRO)]
    ahead_come_l = [msg.coming(x[m].at[OPPOSITE, near:]) for m in range(MICRO)]

    placing = [chosen[m][0] + chosen[m][1] for m in range(MICRO)]

    def dispatch(m):
        block = dot(placing[m], stream[m, :, : KEEP[m]]).astype(BF16).reshape(EXPERTS, CAP, KEEP[m])
        x[m][0, 0] = block[0]
        out[m][...] = block
        for o in ORDER[1:]:
            msg.send(out[m].at[o], x[m].at[0, o], out_leave[m], out_come[m][o], expert=peer[o])

    def dispatch_all(m):
        for rel, at in enumerate(shares[m]):
            block = dot(placing[m], raw[m][rel]).astype(BF16).reshape(EXPERTS, CAP, SHARE[m])
            x_all[m][0, :, at] = block[0]
            out_all[m][:, :, at] = block
            for o in range(1, EXPERTS):
                msg.send(
                    out_all[m].at[o, :, at], x_all[m].at[o, :, at],
                    all_leave[m], all_come[m][rel], expert=peer[o],
                )

    def dispatch_rates():
        total = (ssq[0, 0:1, :] + ssq[1, 0:1, :]) + (ssq[2, 0:1, :] + ssq[3, 0:1, :])
        scales = lax.rsqrt(total * (1.0 / (4 * PART)) + EPS)
        rates_out[...] = jnp.zeros(rates_out.shape, F32)
        for m in range(MICRO):
            scale = scales[:, m * ROWS : (m + 1) * ROWS]
            rate = jnp.sum(placing[m].astype(F32) * scale, axis=1, keepdims=True)
            for o in range(EXPERTS):
                rates_out[o, m : m + 1, :CAP] = flipped(rate[o * CAP : (o + 1) * CAP])
        rates_in[0] = rates_out[0]
        for o in range(1, EXPERTS):
            msg.send(rates_out.at[o], rates_in.at[o], rates_leave, rates_come, expert=peer[o])

    def rates_of(m):
        return jnp.concatenate(
            [flipped(rates_in[o, m : m + 1, :CAP]) for o in range(EXPERTS)], axis=0
        )

    def gather_send(m, pieces):
        for o in pieces:
            if o > 0:
                msg.wait(out_come[m][o])
            msg.send(x[m].at[0, o], x[m].at[RIGHT, o], x_leave_r[m], x_come_r[m][o], tensor=right)
            msg.send(x[m].at[0, o], x[m].at[LEFT, o], x_leave_l[m], x_come_l[m][o], tensor=left)

    def gather_forward(m):
        for i in range(near):
            msg.wait(x_come_r[m][i])
            msg.send(x[m].at[RIGHT, i], x[m].at[OPPOSITE, i], ahead_leave_r[m], ahead_come_r[m], tensor=right)
            o = i + near
            msg.wait(x_come_l[m][o])
            msg.send(x[m].at[LEFT, o], x[m].at[OPPOSITE, o], ahead_leave_l[m], ahead_come_l[m], tensor=left)

    def columns_of(rel, first, width):
        return pl.ds(pl.multiple_of(lax.rem(t + 4 - rel, 4) * PART + first, HS), width)

    def normed_rows(rows, rate, gain):
        return (rows.astype(F32) * rate * gain.astype(F32)).astype(BF16)

    def expert_in(m, rel):
        rows = x[m][rel].reshape(SLOTS, KEEP[m])
        normed = normed_rows(rows, rates_of(m), gains[rel, 0:1, : KEEP[m]])
        value = dot(normed, w13[columns_of(rel, 0, KEEP[m]), :])
        acc[...] = value if rel == 0 else acc[...] + value

    def expert_in_all(m):
        value = None
        for rel in range(4):
            msg.wait(all_come[m][rel])
            rows = x_all[m][:, :, rel * SHARE[m] : (rel + 1) * SHARE[m]].reshape(SLOTS, SHARE[m])
            normed = normed_rows(rows, rates_of(m), gains[rel, 0:1, KEEP[m] :])
            term = dot(normed, w13[columns_of(rel, KEEP[m], SHARE[m]), :])
            value = term if value is None else value + term
        acc[...] += value

    def activate(m):
        gated, lifted = acc[:, :FF], acc[:, FF:]
        hidden[m] = (gated / (1.0 + jnp.exp(-gated)) * lifted).astype(BF16)

    def pairs(buffer, kind):
        return [kind(buffer.at[m]) for m in range(MICRO)]

    def each(buffer, rows):
        return [[msg.coming(buffer.at[m, c, rows]) for c in range(CUTS)] for m in range(MICRO)]

    top, low, every = slice(0, HALF), slice(HALF, SLOTS), slice(None)
    opp_leave, going_r_leave, going_l_leave = (
        pairs(b, msg.leaving) for b in (opp, going_r, going_l)
    )
    steps_r_leave, steps_l_leave, more_r_leave, more_l_leave = (
        pairs(b, msg.leaving) for b in (steps_r, steps_l, more_r, more_l)
    )
    opp_l_come, opp_r_come = each(opp_l, every), each(opp_r, every)
    sum_l_top, sum_l_low = each(sum_l, top), each(sum_l, low)
    sum_r_top, sum_r_low = each(sum_r, top), each(sum_r, low)
    steps_l_come, steps_r_come = each(steps_from_l, every), each(steps_from_r, every)
    more_l_come, more_r_come = each(more_from_l, every), each(more_from_r, every)

    def part(m, c, rel):
        at = pl.multiple_of(lax.rem(t + rel, 4) * PART + c * WIDE, WIDE)
        return dot(hidden[m], wd[:, pl.ds(at, WIDE)])

    def send_opposite(m, c):
        opp[m, c], step = encoded(part(m, c, OPPOSITE))
        for ref in (steps_r, steps_l, more_r, more_l):
            ref[m, c] = jnp.zeros((8, HALF), F32)
        steps_r[m, c, 0:1] = flipped(step[:HALF])
        steps_l[m, c, 0:1] = flipped(step[HALF:])
        msg.send(opp.at[m, c, top], opp_l.at[m, c], opp_leave[m], opp_l_come[m][c], tensor=right)
        msg.send(opp.at[m, c, low], opp_r.at[m, c], opp_leave[m], opp_r_come[m][c], tensor=left)

    def send_direct(m, c):
        value = part(m, c, RIGHT)
        part_r[m, c] = value[:HALF]
        going_r[m, c, low], step = encoded(value[HALF:])
        steps_r[m, c, 1:2] = flipped(step)
        msg.send(steps_r.at[m, c], steps_from_l.at[m, c], steps_r_leave[m], steps_l_come[m][c], tensor=right)
        msg.send(going_r.at[m, c, low], sum_l.at[m, c, low], going_r_leave[m], sum_l_low[m][c], tensor=right)
        value = part(m, c, LEFT)
        part_l[m, c] = value[HALF:]
        going_l[m, c, top], step = encoded(value[:HALF])
        steps_l[m, c, 1:2] = flipped(step)
        msg.send(steps_l.at[m, c], steps_from_r.at[m, c], steps_l_leave[m], steps_r_come[m][c], tensor=left)
        msg.send(going_l.at[m, c, top], sum_r.at[m, c, top], going_l_leave[m], sum_r_top[m][c], tensor=left)

    def sum_middle(m, c):
        msg.wait(steps_l_come[m][c])
        msg.wait(opp_l_come[m][c])
        value = part_r[m, c] + decoded(opp_l[m, c], flipped(steps_from_l[m, c, 0:1]))
        going_r[m, c, top], step = encoded(value)
        more_r[m, c, 0:1] = flipped(step)
        msg.send(more_r.at[m, c], more_from_l.at[m, c], more_r_leave[m], more_l_come[m][c], tensor=right)
        msg.send(going_r.at[m, c, top], sum_l.at[m, c, top], going_r_leave[m], sum_l_top[m][c], tensor=right)
        msg.wait(steps_r_come[m][c])
        msg.wait(opp_r_come[m][c])
        value = part_l[m, c] + decoded(opp_r[m, c], flipped(steps_from_r[m, c, 0:1]))
        going_l[m, c, low], step = encoded(value)
        more_l[m, c, 0:1] = flipped(step)
        msg.send(more_l.at[m, c], more_from_r.at[m, c], more_l_leave[m], more_r_come[m][c], tensor=left)
        msg.send(going_l.at[m, c, low], sum_r.at[m, c, low], going_l_leave[m], sum_r_low[m][c], tensor=left)

    eo_leave = [msg.leaving(eo.at[m, :, 1:]) for m in range(MICRO)]
    ret_come = [[msg.coming(ret.at[m, c, 1:]) for c in range(CUTS)] for m in range(MICRO)]

    def sum_last(m, c):
        for found in (sum_l_low, sum_r_top, more_l_come, sum_l_top, more_r_come, sum_r_low):
            msg.wait(found[m][c])
        above = own[m, c, top] + (
            decoded(sum_l[m, c, top], flipped(more_from_l[m, c, 0:1]))
            + decoded(sum_r[m, c, top], flipped(steps_from_r[m, c, 1:2]))
        )
        below = own[m, c, low] + (
            decoded(sum_l[m, c, low], flipped(steps_from_l[m, c, 1:2]))
            + decoded(sum_r[m, c, low], flipped(more_from_r[m, c, 0:1]))
        )
        value = jnp.concatenate([above.astype(BF16), below.astype(BF16)], axis=0)
        value = value.reshape(EXPERTS, CAP, WIDE)
        ret[m, c, 0] = value[0]
        eo[m, c] = value
        for o in range(1, EXPERTS):
            msg.send(
                eo.at[m, c, o], ret.at[m, c, o], eo_leave[m], ret_come[m][c],
                expert=lax.rem(e + EXPERTS - o, EXPERTS),
            )

    mixed_leave = [msg.leaving(mixed.at[m]) for m in range(MICRO)]
    moe_writes = []
    shift_come = [[msg.coming(rows_in.at[m, 0, c]) for c in range(CUTS)] for m in range(MICRO)]

    def combine(m, c):
        msg.wait(ret_come[m][c])
        returned = ret[m, c].reshape(SLOTS, WIDE)
        columns = slice(c * WIDE, (c + 1) * WIDE)
        value = None
        for k in range(2):
            term = flipped(gates[m, k : k + 1, :]) * dot_first(chosen[m][k], returned)
            value = term if value is None else value + term
        mixed[m, c] = (stream[m, :, columns].astype(F32) + value).astype(BF16)
        msg.send(mixed.at[m, c], rows_in.at[m, 0, c], mixed_leave[m], shift_come[m][c], pipe=after)
        number = len(loads) + len(moe_writes)
        moe_writes.append(
            pltpu.make_async_copy(mixed.at[m, c], moe_out.at[m, :, columns], local_sems.at[number])
        )
        moe_writes[-1].start()

    rows_leave = [msg.leaving(rows_in.at[m, 1:]) for m in range(MICRO)]
    rows_come = [[msg.coming(rows_in.at[m, 1:, c]) for c in range(CUTS)] for m in range(MICRO)]

    def rows_send(m, c):
        msg.wait(shift_come[m][c])
        for rel, other in ((OPPOSITE, opposite), (RIGHT, right), (LEFT, left)):
            msg.send(
                rows_in.at[m, 0, c], rows_in.at[m, rel, c], rows_leave[m], rows_come[m][c], tensor=other
            )

    kv_leave = [msg.leaving(kv_in.at[m, 1:]) for m in range(MICRO)]
    kv_come = [msg.coming(kv_in.at[m, 1:]) for m in range(MICRO)]

    def turned(value):
        swapped = pltpu.roll(value, HS // 2, 1)
        return (value * rope[:, :HS] + swapped * rope[:, HS:]).astype(BF16)

    def project(m):
        for c in range(CUTS):
            msg.wait(rows_come[m][c])
        total = None
        for rel in range(4):
            for c in range(CUTS):
                value = rows_in[m, rel, c].astype(F32)
                term = jnp.sum(value * value, axis=-1, keepdims=True)
                total = term if total is None else total + term
        scale = lax.rsqrt(total * (1.0 / (4 * PART)) + EPS)
        result = None
        for rel in range(4):
            for c in range(CUTS):
                gain = gains[rel, 8:9, c * WIDE : (c + 1) * WIDE].astype(F32)
                normed = (rows_in[m, rel, c].astype(F32) * scale * gain).astype(BF16)
                at = pl.multiple_of(lax.rem(t + 4 - rel, 4) * PART + c * WIDE, WIDE)
                term = dot(normed, wqkv[pl.ds(at, WIDE), :])
                result = term if result is None else result + term
        query = turned(result[:, :HS])
        key = turned(result[:, HS : 2 * HS])
        kv = jnp.concatenate([key, result[:, 2 * HS :].astype(BF16)], axis=1)
        kv_own[m] = kv
        kv_in[m, 0] = kv
        for o in range(1, EXPERTS):
            msg.send(kv_own.at[m], kv_in.at[m, o], kv_leave[m], kv_come[m], expert=peer[o])
        return query

    def attend(m, query):
        column = lax.broadcasted_iota(jnp.int32, (ROWS, LENGTH), 1)
        source = e - column // ROWS
        source = jnp.where(source < 0, source + EXPERTS, source)
        row = e * ROWS + lax.broadcasted_iota(jnp.int32, (ROWS, LENGTH), 0)
        causal = source * ROWS + column % ROWS <= row
        msg.wait(kv_come[m])
        kv = kv_in[m].reshape(LENGTH, 2 * HS)
        scores = lax.dot_general(
            query, kv[:, :HS], (((1,), (1,)), ((), ())), preferred_element_type=F32
        )
        scores = jnp.where(causal, scores * HS ** (-0.5), NEGATIVE)
        highest = jnp.max(scores, axis=-1, keepdims=True)
        weights = jnp.where(causal, jnp.exp(scores - highest), 0.0)
        total = jnp.sum(weights, axis=-1, keepdims=True)
        context[m] = (dot(weights.astype(BF16), kv[:, HS:]) / total).astype(BF16)

    def split_weights():
        step = 512
        row = lax.broadcasted_iota(jnp.int32, (step // 2, step), 0)
        col = lax.broadcasted_iota(jnp.int32, (step // 2, step), 1)

        def body(i, _):
            block = wkv[pl.ds(pl.multiple_of(i * step, step), step), :]
            to = pl.ds(pl.multiple_of(i * (step // 2), step // 2), step // 2)
            for k in range(2):
                pick = jnp.where(col == 2 * row + k, 1.0, 0.0).astype(BF16)
                wqkv[to, (k + 1) * HS : (k + 2) * HS] = dot(pick, block).astype(BF16)
            return 0

        lax.fori_loop(0, wkv.shape[0] // step, body, 0)

    raw_come = [to_tensor_peers(raw[0])]
    dispatch(0)
    gather_send(0, [0])
    dispatch(1)
    ssq_come = to_tensor_peers(ssq)
    raw_come.append(to_tensor_peers(raw[1]))
    gains_come = to_tensor_peers(gains)
    msg.wait(raw_come[0])
    dispatch_all(0)
    gather_send(0, ORDER[1:5])
    msg.wait(ssq_come)
    dispatch_rates()
    gather_send(0, ORDER[5:])
    gather_forward(0)
    msg.wait(raw_come[1])
    dispatch_all(1)
    gather_send(1, ORDER)
    for load in loads[5:]:
        load.wait()
    msg.wait(rates_come)
    msg.wait(gains_come)
    expert_in(0, 0)
    msg.wait(x_come_r[0][near])
    expert_in(0, RIGHT)
    msg.wait(x_come_l[0][0])
    expert_in(0, LEFT)
    msg.wait(ahead_come_r[0])
    msg.wait(ahead_come_l[0])
    expert_in(0, OPPOSITE)
    expert_in_all(0)
    activate(0)
    for c in range(CUTS):
        send_opposite(0, c)
        send_direct(0, c)
    gather_forward(1)
    for c in range(CUTS):
        own[0, c] = part(0, c, 0)
        sum_middle(0, c)
    expert_in(1, 0)
    split_weights()
    msg.wait(x_come_r[1][near])
    expert_in(1, RIGHT)
    msg.wait(x_come_l[1][0])
    expert_in(1, LEFT)
    msg.wait(ahead_come_r[1])
    msg.wait(ahead_come_l[1])
    expert_in(1, OPPOSITE)
    expert_in_all(1)
    activate(1)
    send_opposite(1, 0)
    send_direct(1, 0)
    send_opposite(1, 1)
    sum_last(0, 0)
    sum_middle(1, 0)
    send_direct(1, 1)
    sum_last(0, 1)
    for c in range(CUTS):
        own[1, c] = part(1, c, 0)
    sum_middle(1, 1)
    combine(0, 0)
    combine(0, 1)
    sum_last(1, 0)
    rows_send(0, 0)
    rows_send(0, 1)
    sum_last(1, 1)
    combine(1, 0)
    query0 = project(0)
    combine(1, 1)
    rows_send(1, 0)
    rows_send(1, 1)
    attend(0, query0)
    query1 = project(1)
    attend(1, query1)

    writes = [
        pltpu.make_async_copy(context, context_out, local_sems.at[len(loads) + len(moe_writes)])
    ]
    writes[0].start()
    for write in writes + moe_writes:
        write.wait()
    msg.finish()


def per_device(
    stream, expert_ids, expert_gates, moe_gain, w_gate, w_up, w_down, attn_gain, w_query, w_keyval
):
    hbm = pl.BlockSpec(memory_space=pl.ANY)
    slots_cut = (MICRO, CUTS, SLOTS, WIDE)
    half_cut = (MICRO, CUTS, HALF, WIDE)
    scratch = [
        ((MICRO, ROWS, PART), BF16),
        ((MICRO, 2, ROWS), jnp.int32),
        ((MICRO, 2, ROWS), F32),
        ((1, PART), BF16),
        ((1, PART), BF16),
        ((4 * PART, 2 * FF), BF16),
        ((FF, 4 * PART), BF16),
        ((4 * PART, 3 * HS), BF16),
        ((8 * PART, HS), BF16),
        ((ROWS, 2 * HS), F32),
        ((4, 8, MICRO * ROWS), F32),
        ((4, 16, PART), BF16),
        *(((4, ROWS, SHARE[m]), BF16) for m in range(MICRO)),
        *(((EXPERTS, CAP, KEEP[m]), BF16) for m in range(MICRO)),
        *(((4, EXPERTS, CAP, KEEP[m]), BF16) for m in range(MICRO)),
        *(((EXPERTS, CAP, 4 * SHARE[m]), BF16) for m in (0, 1, 0, 1)),
        ((EXPERTS, 8, HS), F32),
        ((EXPERTS, 8, HS), F32),
        ((SLOTS, 2 * FF), F32),
        ((MICRO, SLOTS, FF), BF16),
        (slots_cut, I16),
        (slots_cut, I16),
        (slots_cut, I16),
        (half_cut, F32),
        (half_cut, F32),
        (slots_cut, F32),
        (half_cut, I16),
        (half_cut, I16),
        (slots_cut, I16),
        (slots_cut, I16),
    ]
    scratch += [((MICRO, CUTS, 8, HALF), F32)] * 8
    scratch += [
        ((MICRO, CUTS, EXPERTS, CAP, WIDE), BF16),
        ((MICRO, CUTS, EXPERTS, CAP, WIDE), BF16),
        ((MICRO, CUTS, ROWS, WIDE), BF16),
        ((MICRO, 4, CUTS, ROWS, WIDE), BF16),
        ((MICRO, ROWS, 2 * HS), BF16),
        ((MICRO, EXPERTS, ROWS, 2 * HS), BF16),
        ((MICRO, ROWS, HS), BF16),
    ]
    moe, context = pl.pallas_call(
        kernel,
        out_shape=(
            jax.ShapeDtypeStruct((MICRO, ROWS, PART), BF16),
            jax.ShapeDtypeStruct((MICRO, ROWS, HS), BF16),
        ),
        in_specs=[hbm] * 11,
        out_specs=(hbm, hbm),
        scratch_shapes=[pltpu.VMEM(shape, kind) for shape, kind in scratch]
        + [pltpu.SemaphoreType.DMA((16,)), pltpu.SemaphoreType.DMA((SEMAPHORES,))],
        compiler_params=pltpu.CompilerParams(
            collective_id=0, has_side_effects=True, vmem_limit_bytes=56 * 1024 * 1024
        ),
        cost_estimate=pl.CostEstimate(
            flops=5_300_000_000, bytes_accessed=13_000_000, transcendentals=500_000
        ),
    )(
        stream[0],
        jnp.transpose(expert_ids[0], (0, 2, 1)),
        jnp.transpose(expert_gates[0], (0, 2, 1)),
        moe_gain,
        attn_gain,
        w_gate[0, 0],
        w_up[0, 0],
        w_down[0, 0],
        w_query[0],
        w_keyval[0].reshape(8 * PART, HS),
        jnp.asarray(rope_table(LENGTH)),
    )
    return moe[None], context[None]


def solution(mesh):
    placed = (
        P("pipe", None, "expert", "tensor"),
        P("pipe", None, "expert", None),
        P("pipe", None, "expert", None),
        P("pipe", "tensor"),
        P("pipe", "expert", None, "tensor"),
        P("pipe", "expert", None, "tensor"),
        P("pipe", "expert", "tensor", None),
        P("pipe", "tensor"),
        P("pipe", None, "tensor"),
        P("pipe", None, None, "tensor"),
    )
    return jax.shard_map(
        per_device,
        mesh=mesh,
        in_specs=placed,
        out_specs=(P("pipe", None, "expert", "tensor"), P("pipe", None, "expert", "tensor")),
        check_vma=False,
    )
```

```python
import jax
import jax.numpy as jnp
import numpy as np
from jax import lax
from jax.experimental import pallas as pl
from jax.experimental.pallas import tpu as pltpu
from jax.sharding import PartitionSpec as P

MESH = pl.DeviceIdType.MESH
HS = 128
EPS = 1e-05
THETA = 1000000.0
NEGATIVE = -1e30
F32 = jnp.float32
BF16 = jnp.bfloat16
I16 = jnp.int16

MICRO = 2
ROWS = 64
PART = 1024
CAP = 32
EXPERTS = 8
SLOTS = EXPERTS * CAP
HALF = SLOTS // 2
CUTS = 2
WIDE = PART // CUTS
SHARE = (384, 768)
KEEP = tuple(PART - share for share in SHARE)
FF = 384
LENGTH = EXPERTS * ROWS
RIGHT, OPPOSITE, LEFT = 1, 2, 3
SEMAPHORES = 140
ORDER = (0, 4, 1, 5, 2, 6, 3, 7)


def rope_table(length):
    freqs = THETA ** (-2.0 * np.arange(HS // 2) / HS)
    angles = np.arange(length)[:, None] * freqs[None, :]
    cosine, sine = np.cos(angles), np.sin(angles)
    return np.concatenate([cosine, cosine, -sine, sine], axis=1).astype(np.float32)


class Group:
    def __init__(self, sem, whole):
        self.sem, self.whole, self.sent, self.waited = sem, whole, False, False


class Messages:
    def __init__(self, sems):
        self.sems, self.used, self.sends, self.recvs = sems, 0, [], []

    def group(self, whole, kind):
        found = Group(self.sems.at[self.used], whole)
        self.used += 1
        kind.append(found)
        return found

    def leaving(self, whole):
        return self.group(whole, self.sends)

    def coming(self, whole):
        return self.group(whole, self.recvs)

    def send(self, src, dst, leaving, coming, **where):
        pltpu.make_async_remote_copy(
            src_ref=src,
            dst_ref=dst,
            send_sem=leaving.sem,
            recv_sem=coming.sem,
            device_id=where,
            device_id_type=MESH,
        ).start()
        leaving.sent = coming.sent = True

    def _any(self, found):
        return pltpu.make_async_remote_copy(
            src_ref=found.whole,
            dst_ref=found.whole,
            send_sem=found.sem,
            recv_sem=found.sem,
            device_id={"tensor": lax.rem(lax.axis_index("tensor") + 1, 4)},
            device_id_type=MESH,
        )

    def wait(self, found):
        self._any(found).wait_recv()
        found.waited = True

    def finish(self):
        for found in self.recvs:
            if found.sent and not found.waited:
                self.wait(found)
        for found in self.sends:
            if found.sent:
                self._any(found).wait_send()


def dot(a, b):
    return jnp.dot(a, b, preferred_element_type=F32)


def dot_first(a, b):
    return lax.dot_general(a, b, (((0,), (0,)), ((), ())), preferred_element_type=F32)


def flipped(line):
    n = max(line.shape)
    diagonal = lax.broadcasted_iota(jnp.int32, (n, n), 0) == lax.broadcasted_iota(
        jnp.int32, (n, n), 1
    )
    axis = 0 if line.shape[1] == 1 else 1
    return jnp.sum(jnp.where(diagonal, line, 0.0), axis=axis, keepdims=True)


def encoded(value):
    highest = jnp.maximum(jnp.max(jnp.abs(value), axis=1, keepdims=True), 1e-30)
    codes = jnp.round(value * (32760.0 / highest)).astype(jnp.int32).astype(I16)
    return codes, highest * (1.0 / 32760.0)


def decoded(codes, step):
    return codes.astype(jnp.int32).astype(F32) * step


def kernel(
    stream_hbm, ids_hbm, gates_hbm, mgain_hbm, again_hbm,
    wg_hbm, wu_hbm, wd_hbm, wq_hbm, wkv_hbm, rope_hbm,
    moe_out, context_out,
    stream, ids, gates, mgain, again, w13, wd, wqkv, wkv, rope,
    ssq, gains, raw0, raw1, out0, out1, x0, x1, out_all0, out_all1, x_all0, x_all1, rates_out, rates_in, acc, hidden,
    opp, going_r, going_l, part_r, part_l, own, opp_l, opp_r, sum_l, sum_r,
    steps_r, steps_l, steps_from_r, steps_from_l, more_r, more_l, more_from_r, more_from_l,
    eo, ret, mixed, rows_in, kv_own, kv_in, context,
    local_sems, sems,
):
    e, t, p = lax.axis_index("expert"), lax.axis_index("tensor"), lax.axis_index("pipe")
    right, left, opposite = lax.rem(t + 1, 4), lax.rem(t + 3, 4), lax.rem(t + 2, 4)
    after, before = lax.rem(p + 1, 8), lax.rem(p + 7, 8)
    peer = [lax.rem(e + o, EXPERTS) for o in range(EXPERTS)]
    msg = Messages(sems)
    raw, out, x = (raw0, raw1), (out0, out1), (x0, x1)
    out_all, x_all = (out_all0, out_all1), (x_all0, x_all1)

    here = pl.ds(pl.multiple_of(e * ROWS, ROWS), ROWS)
    loads = [
        (stream_hbm, stream),
        (ids_hbm, ids),
        (mgain_hbm, mgain),
        (gates_hbm, gates),
        (again_hbm, again),
        (wg_hbm, w13.at[:, :FF]),
        (wu_hbm, w13.at[:, FF:]),
        (wd_hbm, wd),
        (wq_hbm, wqkv.at[:, :HS]),
        (wkv_hbm, wkv),
        (rope_hbm.at[here], rope),
    ]
    loads = [pltpu.make_async_copy(s, d, local_sems.at[i]) for i, (s, d) in enumerate(loads)]
    for load in loads:
        load.start()

    barrier = pltpu.get_barrier_semaphore()
    peers = [{"expert": other} for other in peer[1:]]
    peers += [{"tensor": other} for other in (right, left, opposite)]
    peers += [{"pipe": other} for other in (after, before)]
    for other in peers:
        pl.semaphore_signal(barrier, inc=1, device_id=other, device_id_type=MESH)

    slot = lax.broadcasted_iota(jnp.int32, (SLOTS, ROWS), 0)
    group, place = slot // CAP, slot % CAP
    expert_of = jnp.where(group + e >= EXPERTS, group + e - EXPERTS, group + e)
    row_of = lax.broadcasted_iota(jnp.int32, (ROWS, ROWS), 0)
    col_of = lax.broadcasted_iota(jnp.int32, (ROWS, ROWS), 1)
    earlier = jnp.where(row_of < col_of, 1.0, 0.0).astype(BF16)
    for load in loads[:5]:
        load.wait()
    chosen = []
    for m in range(MICRO):
        first = ids[m, 0:1, :] == expert_of
        second = ids[m, 1:2, :] == expert_of
        named = jnp.where(first | second, 1.0, 0.0)
        taken = dot(named.astype(BF16), earlier) == place.astype(F32)
        chosen.append(
            [jnp.where(which & taken, 1.0, 0.0).astype(BF16) for which in (first, second)]
        )

    value = stream[...].reshape(MICRO * ROWS, PART).astype(F32)
    ssq[0] = jnp.broadcast_to(flipped(jnp.sum(value * value, axis=1, keepdims=True)), (8, MICRO * ROWS))
    gains[0, :8] = jnp.broadcast_to(mgain[...], (8, PART))
    gains[0, 8:] = jnp.broadcast_to(again[...], (8, PART))
    for m in range(MICRO):
        raw[m][0] = stream[m, :, KEEP[m] :]

    pl.semaphore_wait(barrier, len(peers))

    def to_tensor_peers(buffer):
        leaving, coming = msg.leaving(buffer.at[1:4]), msg.coming(buffer.at[1:4])
        for rel, other in ((RIGHT, right), (LEFT, left), (OPPOSITE, opposite)):
            msg.send(buffer.at[0], buffer.at[rel], leaving, coming, tensor=other)
        return coming

    out_leave = [msg.leaving(out[m].at[1:]) for m in range(MICRO)]
    out_come = [[None] + [msg.coming(x[m].at[0, o]) for o in range(1, EXPERTS)] for m in range(MICRO)]
    all_leave = [msg.leaving(out_all[m].at[1:]) for m in range(MICRO)]
    all_come = [
        [msg.coming(x_all[m].at[1 : EXPERTS // 2]), msg.coming(x_all[m].at[EXPERTS // 2 :])]
        for m in range(MICRO)
    ]
    rates_leave, rates_come = msg.leaving(rates_out.at[1:]), msg.coming(rates_in.at[1:])
    x_leave_r = [msg.leaving(x[m].at[0]) for m in range(MICRO)]
    x_leave_l = [msg.leaving(x[m].at[0]) for m in range(MICRO)]
    near = EXPERTS // 2
    x_come_r = [
        [msg.coming(x[m].at[RIGHT, o]) for o in range(near)] + [msg.coming(x[m].at[RIGHT, near:])] * near
        for m in range(MICRO)
    ]
    x_come_l = [
        [msg.coming(x[m].at[LEFT, :near])] * near + [msg.coming(x[m].at[LEFT, o]) for o in range(near, EXPERTS)]
        for m in range(MICRO)
    ]
    ahead_leave_r = [msg.leaving(x[m].at[RIGHT, :near]) for m in range(MICRO)]
    ahead_leave_l = [msg.leaving(x[m].at[LEFT, near:]) for m in range(MICRO)]
    ahead_come_r = [msg.coming(x[m].at[OPPOSITE, :near]) for m in range(MICRO)]
    ahead_come_l = [msg.coming(x[m].at[OPPOSITE, near:]) for m in range(MICRO)]

    placing = [chosen[m][0] + chosen[m][1] for m in range(MICRO)]

    def dispatch(m):
        block = dot(placing[m], stream[m, :, : KEEP[m]]).astype(BF16).reshape(EXPERTS, CAP, KEEP[m])
        x[m][0, 0] = block[0]
        out[m][...] = block
        for o in ORDER[1:]:
            msg.send(out[m].at[o], x[m].at[0, o], out_leave[m], out_come[m][o], expert=peer[o])

    def dispatch_all(m):
        for rel in range(4):
            at = slice(rel * SHARE[m], (rel + 1) * SHARE[m])
            block = dot(placing[m], raw[m][rel]).astype(BF16).reshape(EXPERTS, CAP, SHARE[m])
            x_all[m][0, :, at] = block[0]
            out_all[m][:, :, at] = block
        for o in range(1, EXPERTS):
            msg.send(out_all[m].at[o], x_all[m].at[o], all_leave[m], all_come[m][o // (EXPERTS // 2)], expert=peer[o])

    def dispatch_rates():
        total = (ssq[0, 0:1, :] + ssq[1, 0:1, :]) + (ssq[2, 0:1, :] + ssq[3, 0:1, :])
        scales = lax.rsqrt(total * (1.0 / (4 * PART)) + EPS)
        rates_out[...] = jnp.zeros(rates_out.shape, F32)
        for m in range(MICRO):
            scale = scales[:, m * ROWS : (m + 1) * ROWS]
            rate = jnp.sum(placing[m].astype(F32) * scale, axis=1, keepdims=True)
            for o in range(EXPERTS):
                rates_out[o, m : m + 1, :CAP] = flipped(rate[o * CAP : (o + 1) * CAP])
        rates_in[0] = rates_out[0]
        for o in range(1, EXPERTS):
            msg.send(rates_out.at[o], rates_in.at[o], rates_leave, rates_come, expert=peer[o])

    def rates_of(m):
        return jnp.concatenate(
            [flipped(rates_in[o, m : m + 1, :CAP]) for o in range(EXPERTS)], axis=0
        )

    def gather_send(m, pieces):
        for o in pieces:
            if o > 0:
                msg.wait(out_come[m][o])
            msg.send(x[m].at[0, o], x[m].at[RIGHT, o], x_leave_r[m], x_come_r[m][o], tensor=right)
            msg.send(x[m].at[0, o], x[m].at[LEFT, o], x_leave_l[m], x_come_l[m][o], tensor=left)

    def gather_forward(m):
        for i in range(near):
            msg.wait(x_come_r[m][i])
            msg.send(x[m].at[RIGHT, i], x[m].at[OPPOSITE, i], ahead_leave_r[m], ahead_come_r[m], tensor=right)
            o = i + near
            msg.wait(x_come_l[m][o])
            msg.send(x[m].at[LEFT, o], x[m].at[OPPOSITE, o], ahead_leave_l[m], ahead_come_l[m], tensor=left)

    def columns_of(rel, first, width):
        return pl.ds(pl.multiple_of(lax.rem(t + 4 - rel, 4) * PART + first, HS), width)

    def normed_rows(rows, rate, gain):
        return (rows.astype(F32) * rate * gain.astype(F32)).astype(BF16)

    def expert_in(m, rel):
        rows = x[m][rel].reshape(SLOTS, KEEP[m])
        normed = normed_rows(rows, rates_of(m), gains[rel, 0:1, : KEEP[m]])
        value = dot(normed, w13[columns_of(rel, 0, KEEP[m]), :])
        acc[...] = value if rel == 0 else acc[...] + value

    def expert_in_all(m):
        rate = rates_of(m)
        for part_of, slots in enumerate((slice(0, HALF), slice(HALF, SLOTS))):
            blocks = slice(part_of * (EXPERTS // 2), (part_of + 1) * (EXPERTS // 2))
            msg.wait(all_come[m][part_of])
            value = None
            for rel in range(4):
                rows = x_all[m][blocks, :, rel * SHARE[m] : (rel + 1) * SHARE[m]]
                normed = normed_rows(
                    rows.reshape(HALF, SHARE[m]), rate[slots], gains[rel, 0:1, KEEP[m] :]
                )
                term = dot(normed, w13[columns_of(rel, KEEP[m], SHARE[m]), :])
                value = term if value is None else value + term
            acc[slots, :] += value

    def activate(m):
        gated, lifted = acc[:, :FF], acc[:, FF:]
        hidden[m] = (gated / (1.0 + jnp.exp(-gated)) * lifted).astype(BF16)

    def pairs(buffer, kind):
        return [kind(buffer.at[m]) for m in range(MICRO)]

    def each(buffer, rows):
        return [[msg.coming(buffer.at[m, c, rows]) for c in range(CUTS)] for m in range(MICRO)]

    top, low, every = slice(0, HALF), slice(HALF, SLOTS), slice(None)
    opp_leave, going_r_leave, going_l_leave = (
        pairs(b, msg.leaving) for b in (opp, going_r, going_l)
    )
    steps_r_leave, steps_l_leave, more_r_leave, more_l_leave = (
        pairs(b, msg.leaving) for b in (steps_r, steps_l, more_r, more_l)
    )
    opp_l_come, opp_r_come = each(opp_l, every), each(opp_r, every)
    sum_l_top, sum_l_low = each(sum_l, top), each(sum_l, low)
    sum_r_top, sum_r_low = each(sum_r, top), each(sum_r, low)
    steps_l_come, steps_r_come = each(steps_from_l, every), each(steps_from_r, every)
    more_l_come, more_r_come = each(more_from_l, every), each(more_from_r, every)

    def part(m, c, rel):
        at = pl.multiple_of(lax.rem(t + rel, 4) * PART + c * WIDE, WIDE)
        return dot(hidden[m], wd[:, pl.ds(at, WIDE)])

    def send_opposite(m, c):
        opp[m, c], step = encoded(part(m, c, OPPOSITE))
        for ref in (steps_r, steps_l, more_r, more_l):
            ref[m, c] = jnp.zeros((8, HALF), F32)
        steps_r[m, c, 0:1] = flipped(step[:HALF])
        steps_l[m, c, 0:1] = flipped(step[HALF:])
        msg.send(opp.at[m, c, top], opp_l.at[m, c], opp_leave[m], opp_l_come[m][c], tensor=right)
        msg.send(opp.at[m, c, low], opp_r.at[m, c], opp_leave[m], opp_r_come[m][c], tensor=left)

    def send_direct(m, c):
        value = part(m, c, RIGHT)
        part_r[m, c] = value[:HALF]
        going_r[m, c, low], step = encoded(value[HALF:])
        steps_r[m, c, 1:2] = flipped(step)
        msg.send(steps_r.at[m, c], steps_from_l.at[m, c], steps_r_leave[m], steps_l_come[m][c], tensor=right)
        msg.send(going_r.at[m, c, low], sum_l.at[m, c, low], going_r_leave[m], sum_l_low[m][c], tensor=right)
        value = part(m, c, LEFT)
        part_l[m, c] = value[HALF:]
        going_l[m, c, top], step = encoded(value[:HALF])
        steps_l[m, c, 1:2] = flipped(step)
        msg.send(steps_l.at[m, c], steps_from_r.at[m, c], steps_l_leave[m], steps_r_come[m][c], tensor=left)
        msg.send(going_l.at[m, c, top], sum_r.at[m, c, top], going_l_leave[m], sum_r_top[m][c], tensor=left)

    def sum_middle(m, c):
        msg.wait(steps_l_come[m][c])
        msg.wait(opp_l_come[m][c])
        value = part_r[m, c] + decoded(opp_l[m, c], flipped(steps_from_l[m, c, 0:1]))
        going_r[m, c, top], step = encoded(value)
        more_r[m, c, 0:1] = flipped(step)
        msg.send(more_r.at[m, c], more_from_l.at[m, c], more_r_leave[m], more_l_come[m][c], tensor=right)
        msg.send(going_r.at[m, c, top], sum_l.at[m, c, top], going_r_leave[m], sum_l_top[m][c], tensor=right)
        msg.wait(steps_r_come[m][c])
        msg.wait(opp_r_come[m][c])
        value = part_l[m, c] + decoded(opp_r[m, c], flipped(steps_from_r[m, c, 0:1]))
        going_l[m, c, low], step = encoded(value)
        more_l[m, c, 0:1] = flipped(step)
        msg.send(more_l.at[m, c], more_from_r.at[m, c], more_l_leave[m], more_r_come[m][c], tensor=left)
        msg.send(going_l.at[m, c, low], sum_r.at[m, c, low], going_l_leave[m], sum_r_low[m][c], tensor=left)

    eo_leave = [msg.leaving(eo.at[m, :, 1:]) for m in range(MICRO)]
    ret_come = [[msg.coming(ret.at[m, c, 1:]) for c in range(CUTS)] for m in range(MICRO)]

    def sum_last(m, c):
        for found in (sum_l_low, sum_r_top, more_l_come, sum_l_top, more_r_come, sum_r_low):
            msg.wait(found[m][c])
        above = own[m, c, top] + (
            decoded(sum_l[m, c, top], flipped(more_from_l[m, c, 0:1]))
            + decoded(sum_r[m, c, top], flipped(steps_from_r[m, c, 1:2]))
        )
        below = own[m, c, low] + (
            decoded(sum_l[m, c, low], flipped(steps_from_l[m, c, 1:2]))
            + decoded(sum_r[m, c, low], flipped(more_from_r[m, c, 0:1]))
        )
        value = jnp.concatenate([above.astype(BF16), below.astype(BF16)], axis=0)
        value = value.reshape(EXPERTS, CAP, WIDE)
        ret[m, c, 0] = value[0]
        eo[m, c] = value
        for o in range(1, EXPERTS):
            msg.send(
                eo.at[m, c, o], ret.at[m, c, o], eo_leave[m], ret_come[m][c],
                expert=lax.rem(e + EXPERTS - o, EXPERTS),
            )

    mixed_leave = [msg.leaving(mixed.at[m]) for m in range(MICRO)]
    moe_writes = []
    shift_come = [[msg.coming(rows_in.at[m, 0, c]) for c in range(CUTS)] for m in range(MICRO)]

    def combine(m, c):
        msg.wait(ret_come[m][c])
        returned = ret[m, c].reshape(SLOTS, WIDE)
        columns = slice(c * WIDE, (c + 1) * WIDE)
        value = None
        for k in range(2):
            term = flipped(gates[m, k : k + 1, :]) * dot_first(chosen[m][k], returned)
            value = term if value is None else value + term
        mixed[m, c] = (stream[m, :, columns].astype(F32) + value).astype(BF16)
        msg.send(mixed.at[m, c], rows_in.at[m, 0, c], mixed_leave[m], shift_come[m][c], pipe=after)
        number = len(loads) + len(moe_writes)
        moe_writes.append(
            pltpu.make_async_copy(mixed.at[m, c], moe_out.at[m, :, columns], local_sems.at[number])
        )
        moe_writes[-1].start()

    rows_leave = [msg.leaving(rows_in.at[m, 1:]) for m in range(MICRO)]
    rows_come = [[msg.coming(rows_in.at[m, 1:, c]) for c in range(CUTS)] for m in range(MICRO)]

    def rows_send(m, c):
        msg.wait(shift_come[m][c])
        for rel, other in ((OPPOSITE, opposite), (RIGHT, right), (LEFT, left)):
            msg.send(
                rows_in.at[m, 0, c], rows_in.at[m, rel, c], rows_leave[m], rows_come[m][c], tensor=other
            )

    kv_leave = [msg.leaving(kv_in.at[m, 1:]) for m in range(MICRO)]
    kv_come = [msg.coming(kv_in.at[m, 1:]) for m in range(MICRO)]

    def turned(value):
        swapped = pltpu.roll(value, HS // 2, 1)
        return (value * rope[:, :HS] + swapped * rope[:, HS:]).astype(BF16)

    def project(m):
        for c in range(CUTS):
            msg.wait(rows_come[m][c])
        total = None
        for rel in range(4):
            for c in range(CUTS):
                value = rows_in[m, rel, c].astype(F32)
                term = jnp.sum(value * value, axis=-1, keepdims=True)
                total = term if total is None else total + term
        scale = lax.rsqrt(total * (1.0 / (4 * PART)) + EPS)
        result = None
        for rel in range(4):
            for c in range(CUTS):
                gain = gains[rel, 8:9, c * WIDE : (c + 1) * WIDE].astype(F32)
                normed = (rows_in[m, rel, c].astype(F32) * scale * gain).astype(BF16)
                at = pl.multiple_of(lax.rem(t + 4 - rel, 4) * PART + c * WIDE, WIDE)
                term = dot(normed, wqkv[pl.ds(at, WIDE), :])
                result = term if result is None else result + term
        query = turned(result[:, :HS])
        key = turned(result[:, HS : 2 * HS])
        kv = jnp.concatenate([key, result[:, 2 * HS :].astype(BF16)], axis=1)
        kv_own[m] = kv
        kv_in[m, 0] = kv
        for o in range(1, EXPERTS):
            msg.send(kv_own.at[m], kv_in.at[m, o], kv_leave[m], kv_come[m], expert=peer[o])
        return query

    def attend(m, query):
        column = lax.broadcasted_iota(jnp.int32, (ROWS, LENGTH), 1)
        source = e - column // ROWS
        source = jnp.where(source < 0, source + EXPERTS, source)
        row = e * ROWS + lax.broadcasted_iota(jnp.int32, (ROWS, LENGTH), 0)
        causal = source * ROWS + column % ROWS <= row
        msg.wait(kv_come[m])
        kv = kv_in[m].reshape(LENGTH, 2 * HS)
        scores = lax.dot_general(
            query, kv[:, :HS], (((1,), (1,)), ((), ())), preferred_element_type=F32
        )
        scores = jnp.where(causal, scores * HS ** (-0.5), NEGATIVE)
        highest = jnp.max(scores, axis=-1, keepdims=True)
        weights = jnp.where(causal, jnp.exp(scores - highest), 0.0)
        total = jnp.sum(weights, axis=-1, keepdims=True)
        context[m] = (dot(weights.astype(BF16), kv[:, HS:]) / total).astype(BF16)

    def split_weights():
        step = 512
        row = lax.broadcasted_iota(jnp.int32, (step // 2, step), 0)
        col = lax.broadcasted_iota(jnp.int32, (step // 2, step), 1)

        def body(i, _):
            block = wkv[pl.ds(pl.multiple_of(i * step, step), step), :]
            to = pl.ds(pl.multiple_of(i * (step // 2), step // 2), step // 2)
            for k in range(2):
                pick = jnp.where(col == 2 * row + k, 1.0, 0.0).astype(BF16)
                wqkv[to, (k + 1) * HS : (k + 2) * HS] = dot(pick, block).astype(BF16)
            return 0

        lax.fori_loop(0, wkv.shape[0] // step, body, 0)

    raw_come = [to_tensor_peers(raw[0])]
    dispatch(0)
    gather_send(0, [0])
    dispatch(1)
    ssq_come = to_tensor_peers(ssq)
    raw_come.append(to_tensor_peers(raw[1]))
    gains_come = to_tensor_peers(gains)
    msg.wait(raw_come[0])
    dispatch_all(0)
    gather_send(0, ORDER[1:5])
    msg.wait(ssq_come)
    dispatch_rates()
    gather_send(0, ORDER[5:])
    gather_forward(0)
    msg.wait(raw_come[1])
    dispatch_all(1)
    gather_send(1, ORDER)
    for load in loads[5:]:
        load.wait()
    msg.wait(rates_come)
    msg.wait(gains_come)
    expert_in(0, 0)
    msg.wait(x_come_r[0][near])
    expert_in(0, RIGHT)
    msg.wait(x_come_l[0][0])
    expert_in(0, LEFT)
    msg.wait(ahead_come_r[0])
    msg.wait(ahead_come_l[0])
    expert_in(0, OPPOSITE)
    expert_in_all(0)
    activate(0)
    for c in range(CUTS):
        send_opposite(0, c)
        send_direct(0, c)
    gather_forward(1)
    for c in range(CUTS):
        own[0, c] = part(0, c, 0)
        sum_middle(0, c)
    expert_in(1, 0)
    split_weights()
    msg.wait(x_come_r[1][near])
    expert_in(1, RIGHT)
    msg.wait(x_come_l[1][0])
    expert_in(1, LEFT)
    msg.wait(ahead_come_r[1])
    msg.wait(ahead_come_l[1])
    expert_in(1, OPPOSITE)
    expert_in_all(1)
    activate(1)
    send_opposite(1, 0)
    send_direct(1, 0)
    send_opposite(1, 1)
    sum_last(0, 0)
    sum_middle(1, 0)
    send_direct(1, 1)
    sum_last(0, 1)
    for c in range(CUTS):
        own[1, c] = part(1, c, 0)
    sum_middle(1, 1)
    combine(0, 0)
    combine(0, 1)
    sum_last(1, 0)
    rows_send(0, 0)
    rows_send(0, 1)
    sum_last(1, 1)
    combine(1, 0)
    query0 = project(0)
    combine(1, 1)
    rows_send(1, 0)
    rows_send(1, 1)
    attend(0, query0)
    query1 = project(1)
    attend(1, query1)

    writes = [
        pltpu.make_async_copy(context, context_out, local_sems.at[len(loads) + len(moe_writes)])
    ]
    writes[0].start()
    for write in writes + moe_writes:
        write.wait()
    msg.finish()


def per_device(
    stream, expert_ids, expert_gates, moe_gain, w_gate, w_up, w_down, attn_gain, w_query, w_keyval
):
    hbm = pl.BlockSpec(memory_space=pl.ANY)
    slots_cut = (MICRO, CUTS, SLOTS, WIDE)
    half_cut = (MICRO, CUTS, HALF, WIDE)
    scratch = [
        ((MICRO, ROWS, PART), BF16),
        ((MICRO, 2, ROWS), jnp.int32),
        ((MICRO, 2, ROWS), F32),
        ((1, PART), BF16),
        ((1, PART), BF16),
        ((4 * PART, 2 * FF), BF16),
        ((FF, 4 * PART), BF16),
        ((4 * PART, 3 * HS), BF16),
        ((8 * PART, HS), BF16),
        ((ROWS, 2 * HS), F32),
        ((4, 8, MICRO * ROWS), F32),
        ((4, 16, PART), BF16),
        *(((4, ROWS, SHARE[m]), BF16) for m in range(MICRO)),
        *(((EXPERTS, CAP, KEEP[m]), BF16) for m in range(MICRO)),
        *(((4, EXPERTS, CAP, KEEP[m]), BF16) for m in range(MICRO)),
        *(((EXPERTS, CAP, 4 * SHARE[m]), BF16) for m in (0, 1, 0, 1)),
        ((EXPERTS, 8, HS), F32),
        ((EXPERTS, 8, HS), F32),
        ((SLOTS, 2 * FF), F32),
        ((MICRO, SLOTS, FF), BF16),
        (slots_cut, I16),
        (slots_cut, I16),
        (slots_cut, I16),
        (half_cut, F32),
        (half_cut, F32),
        (slots_cut, F32),
        (half_cut, I16),
        (half_cut, I16),
        (slots_cut, I16),
        (slots_cut, I16),
    ]
    scratch += [((MICRO, CUTS, 8, HALF), F32)] * 8
    scratch += [
        ((MICRO, CUTS, EXPERTS, CAP, WIDE), BF16),
        ((MICRO, CUTS, EXPERTS, CAP, WIDE), BF16),
        ((MICRO, CUTS, ROWS, WIDE), BF16),
        ((MICRO, 4, CUTS, ROWS, WIDE), BF16),
        ((MICRO, ROWS, 2 * HS), BF16),
        ((MICRO, EXPERTS, ROWS, 2 * HS), BF16),
        ((MICRO, ROWS, HS), BF16),
    ]
    moe, context = pl.pallas_call(
        kernel,
        out_shape=(
            jax.ShapeDtypeStruct((MICRO, ROWS, PART), BF16),
            jax.ShapeDtypeStruct((MICRO, ROWS, HS), BF16),
        ),
        in_specs=[hbm] * 11,
        out_specs=(hbm, hbm),
        scratch_shapes=[pltpu.VMEM(shape, kind) for shape, kind in scratch]
        + [pltpu.SemaphoreType.DMA((16,)), pltpu.SemaphoreType.DMA((SEMAPHORES,))],
        compiler_params=pltpu.CompilerParams(
            collective_id=0, has_side_effects=True, vmem_limit_bytes=56 * 1024 * 1024
        ),
        cost_estimate=pl.CostEstimate(
            flops=5_300_000_000, bytes_accessed=13_000_000, transcendentals=500_000
        ),
    )(
        stream[0],
        jnp.transpose(expert_ids[0], (0, 2, 1)),
        jnp.transpose(expert_gates[0], (0, 2, 1)),
        moe_gain,
        attn_gain,
        w_gate[0, 0],
        w_up[0, 0],
        w_down[0, 0],
        w_query[0],
        w_keyval[0].reshape(8 * PART, HS),
        jnp.asarray(rope_table(LENGTH)),
    )
    return moe[None], context[None]


def solution(mesh):
    placed = (
        P("pipe", None, "expert", "tensor"),
        P("pipe", None, "expert", None),
        P("pipe", None, "expert", None),
        P("pipe", "tensor"),
        P("pipe", "expert", None, "tensor"),
        P("pipe", "expert", None, "tensor"),
        P("pipe", "expert", "tensor", None),
        P("pipe", "tensor"),
        P("pipe", None, "tensor"),
        P("pipe", None, None, "tensor"),
    )
    return jax.shard_map(
        per_device,
        mesh=mesh,
        in_specs=placed,
        out_specs=(P("pipe", None, "expert", "tensor"), P("pipe", None, "expert", "tensor")),
        check_vma=False,
    )
```
